32 devices in a mesh: blk: 8 (over y, x, core), sub: 4 (over z).
Axes of the slice: x: 2, y: 2, z: 4, core: 2. Of those that a mesh axis runs over, the one named last changes fastest.
Arguments:
- vorticity: float32 [3, 8, 32, 1024], P(None, 'blk', 'sub'), may hold values from -6 to 6
- velocity: float32 [3, 8, 32, 1024], P(None, 'blk', 'sub'), may hold values from -0.9 to 0.9
- gradient: float32 [9, 8, 32, 1024], P(None, 'blk', 'sub'), may hold values from -3 to 3
- neighbour: int32 [8, 6], P('blk'), may hold values from 0 to 7, as said below
Outputs:
- new_vorticity: float32 [3, 8, 32, 1024], P(None, 'blk', 'sub')
The draws below stay inside these ranges and needn't reach their ends.
Inputs may be any that keep to these rules, and one draw needn't show every extreme that they name: The blocks form a periodic grid of blocks numbered along a space-filling curve; neighbour[b, 2a] and neighbour[b, 2a + 1] are the blocks beside block b below and above it along dimension a, so neighbour[neighbour[b, 2a], 2a + 1] = b and neighbour[neighbour[b, 2a + 1], 2a] = b.
All inputs are finite; a program needn't handle non-finite values.
Results may differ from the reference program's by a relative error of at most 0.0003.
Values sent between devices are 32-bit elements; how exact they have to be, the bound alone decides.
No kernel may reach another device: no remote copies, remote signals or barrier semaphores. Data moves between devices by JAX's collectives and lax.ppermute only.
A program may use at most 64 MiB of HBM per device.

```python
import jax
import jax.numpy as jnp
from jax import lax

B = 32
NBLK = 8


def draw_neighbour(key, part):
    key = jax.random.fold_in(key, 11)
    bit_count = NBLK.bit_length() - 1
    axis_bits = [(bit_count + 2) // 3, (bit_count + 1) // 3, bit_count // 3]
    grid_size = [2 ** n for n in axis_bits]
    bit_plan = []
    used_bits = [0, 0, 0]
    while len(bit_plan) < bit_count:
        for axis_id in range(3):
            if used_bits[axis_id] < axis_bits[axis_id] and len(bit_plan) < bit_count:
                bit_plan.append((axis_id, used_bits[axis_id]))
                used_bits[axis_id] += 1
    top_axis = bit_plan[-1][0]
    half_size = grid_size[top_axis] // 2
    label_key, order_key = jax.random.split(key)
    relabel = jax.random.randint(label_key, (), 0, NBLK, dtype=jnp.int32)
    axis_order = jax.random.permutation(order_key, 3)

    def reflect(coords):
        result = list(coords)
        upper = coords[top_axis]
        result[top_axis] = jnp.where(upper >= half_size, 3 * half_size - 1 - upper, upper)
        return result

    def encode(where_at):
        folded = reflect(where_at)
        result = jnp.zeros((NBLK,), jnp.int32)
        for bit_level, (axis_id, bit_place) in enumerate(bit_plan):
            result = result + folded[axis_id] // 2 ** bit_place % 2 * 2 ** bit_level
        return jnp.bitwise_xor(result, relabel)
    block_ids = jnp.bitwise_xor(jnp.arange(NBLK, dtype=jnp.int32), relabel)
    folded = [jnp.zeros((NBLK,), jnp.int32) for n in range(3)]
    for bit_level, (axis_id, bit_place) in enumerate(bit_plan):
        folded[axis_id] = folded[axis_id] + block_ids // 2 ** bit_level % 2 * 2 ** bit_place
    coords = reflect(folded)
    per_axis = []
    for axis_id in range(3):
        pair = []
        for toward in (-1, 1):
            moved = list(coords)
            moved[axis_id] = (coords[axis_id] + toward) % grid_size[axis_id]
            pair.append(encode(moved))
        per_axis.append(jnp.stack(pair, axis=0))
    table = jnp.stack(per_axis, axis=0)
    table = jnp.take(table, axis_order, axis=0)
    return table.reshape((6, NBLK)).T.astype(jnp.int32)


def block_scale(key, dims, shards, least, largest):
    def one(position, shards_of):
        draws = jax.random.uniform(jax.random.fold_in(jax.random.fold_in(key, 6), position), (shards_of,), jnp.float32, least / len(shards), largest / len(shards))
        return jnp.repeat(jnp.exp(draws), dims[position] // shards_of).reshape((-1,) + (1,) * (len(dims) - position - 1))

    loudness = one(*shards[0])
    for cut in shards[1:]:
        loudness = loudness * one(*cut)
    return loudness


def gaussian(rng, dims, width, most, cuts=(), kind=jnp.bfloat16):
    array = width * jax.random.normal(rng, dims, jnp.float32)
    if cuts:
        array = array * block_scale(rng, dims, cuts, -0.22, 0.18)
    return jnp.clip(array, -most, most).astype(kind)


def setup_inputs(seed: int = 0) -> dict:
    key_of = jax.random.split(jax.random.key(seed), 5)
    vorticity = gaussian(key_of[0], (3, NBLK, B, B * B), 1.0, 6.0, ((1, 8), (2, 4)), jnp.float32)
    velocity = jnp.clip(jax.random.uniform(key_of[1], (3, NBLK, B, B * B), jnp.float32, -0.9, 0.9) * block_scale(key_of[1], (3, NBLK, B, B * B), ((1, 8), (2, 4)), -0.4, 0.0), -0.9, 0.9)
    gradient = gaussian(key_of[2], (9, NBLK, B, B * B), 0.5, 3.0, ((1, 8), (2, 4)), jnp.float32)
    neighbour = draw_neighbour(jax.random.fold_in(key_of[4], 71), 0)
    return dict(vorticity=vorticity, velocity=velocity, gradient=gradient, neighbour=neighbour)


stretch_step = 0.25


def kernel(offset):
    a = jnp.abs(offset)
    near_part = 1.0 - 2.5 * a * a + 1.5 * a * a * a
    far_part = 0.5 * (2.0 - a) * (2.0 - a) * (1.0 - a)
    return jnp.where(a < 1.0, near_part, jnp.where(a < 2.0, far_part, 0.0))


def spread(values, displace, dim):
    summed = None
    for k in range(-2, 3):
        weighted = values * kernel(k - displace)[None]
        padding = [(0, 0)] * values.ndim
        padding[dim] = (2 + k, 2 - k)
        placed = jnp.pad(weighted, padding)
        summed = placed if summed is None else summed + placed
    return summed


def place_rims(interior, from_above, from_below, dim):
    length = interior.shape[dim]
    upper_pad = [(0, 0)] * interior.ndim
    upper_pad[dim] = (length - 2, 0)
    lower_pad = [(0, 0)] * interior.ndim
    lower_pad[dim] = (0, length - 2)
    return interior + jnp.pad(from_above, upper_pad) + jnp.pad(from_below, lower_pad)


def stretch(w, g):
    return jnp.stack([w[i] + stretch_step * (g[3 * i] * w[0] + g[3 * i + 1] * w[1] + g[3 * i + 2] * w[2]) for i in range(3)])


def remesh_pass(values, displace, neighbour, dim):
    length = values.shape[dim]
    summed = spread(values, displace, dim)
    interior = lax.slice_in_dim(summed, 2, length + 2, axis=dim)
    lower_spill = lax.slice_in_dim(summed, 0, 2, axis=dim)
    upper_spill = lax.slice_in_dim(summed, length + 2, length + 4, axis=dim)
    face_id = 2 * (dim - 2)
    from_above = jnp.take(lower_spill, neighbour[:, face_id + 1], axis=1)
    from_below = jnp.take(upper_spill, neighbour[:, face_id], axis=1)
    return place_rims(interior, from_above, from_below, dim)


def reference(vorticity, velocity, gradient, neighbour):
    block_shape = (NBLK, B, B, B)
    w = vorticity.reshape((3,) + block_shape)
    u = velocity.reshape((3,) + block_shape)
    g = gradient.reshape((9,) + block_shape)
    values = stretch(w, g)
    for dim in (2, 3, 4):
        values = remesh_pass(values, u[dim - 2], neighbour, dim)
    return values.reshape(vorticity.shape)
```

```python
import functools

import jax
import jax.numpy as jnp
from jax import lax
from jax.experimental import pallas as pl
from jax.experimental.pallas import tpu as pltpu
from jax.sharding import PartitionSpec as P

B = 32
TILES = B * B // 128
stretch_step = 0.25

AFTER_Y, AFTER_Z, U1_Y, U1_Z, U2_Z = 0, 3, 6, 7, 8
FACES = 9
NEAR_Y, NEAR_Z = 9, 10
FAR, FAR_Y, FAR_Z = 11, 19, 20
SENT = 21


def iotas():
    return (
        lax.broadcasted_iota(jnp.int32, (8, 128), 0),
        lax.broadcasted_iota(jnp.int32, (8, 128), 1),
    )


def weights(u):
    a = jnp.abs(u)
    rest = 1.0 - a
    centre = 1.0 + a * a * (1.5 * a - 2.5)
    toward = a * (0.5 + a * (2.0 - 1.5 * a))
    away = -0.5 * a * rest * rest
    far = -0.5 * a * a * rest
    up = u >= 0.0
    return {
        0: centre,
        1: jnp.where(up, toward, away),
        -1: jnp.where(up, away, toward),
        2: jnp.where(up, far, 0.0),
        -2: jnp.where(up, 0.0, far),
    }


def lane(tile):
    return pl.ds(128 * tile, 128)


def y_face(tiles, lanes):
    return jnp.where(lanes < 64, tiles[0], tiles[TILES - 1])


def z_face(tiles, lanes):
    m = lanes & 3
    index = 32 * ((lanes >> 2) & 3) + jnp.where(m < 2, m, 28 + m)
    face = None
    for t, tile in enumerate(tiles):
        picked = jnp.take_along_axis(tile, index, axis=1)
        face = picked if face is None else jnp.where((lanes >> 4) == t, picked, face)
    return face


def first_kernel(slab, nb_ref, w_ref, u_ref, g_ref, after_ref, face_ref, near_ref, far_ref):
    rows, lanes = iotas()
    odd = lax.axis_index("sub") % 2 == 1
    meta = jnp.zeros((8, 128), jnp.float32)
    for j in range(6):
        meta = jnp.where(lanes == j, nb_ref[0, j].astype(jnp.float32), meta)
    after = [[], [], []]
    near, far = [], []
    for t in range(TILES):
        w = [w_ref[c, 0, :, lane(t)] for c in range(3)]
        weight = weights(u_ref[0, 0, :, lane(t)])
        ups, downs = [], []
        for c in range(3):
            q = w[c] + stretch_step * (
                g_ref[3 * c, 0, :, lane(t)] * w[0]
                + g_ref[3 * c + 1, 0, :, lane(t)] * w[1]
                + g_ref[3 * c + 2, 0, :, lane(t)] * w[2]
            )
            inside, up, down = q * weight[0], 0.0, 0.0
            for k in (1, 2):
                moved = pltpu.roll(q * weight[k], k, 0)
                spilt = rows < k if slab == 8 else rows >= slab
                inside = inside + jnp.where(spilt, 0.0, moved)
                up = up + jnp.where(spilt, moved, 0.0)
                moved = pltpu.roll(q * weight[-k], 8 - k, 0)
                spilt = rows >= 8 - k
                inside = inside + jnp.where(spilt, 0.0, moved)
                down = down + jnp.where(spilt, moved, 0.0)
            after[c].append(inside)
            after_ref[c, :, lane(t)] = inside
            ups.append(up)
            downs.append(down)
        rest = meta if t == 0 else 0.0
        packed_up, packed_down = rest, rest
        for c in (2, 1, 0):
            here = rows < 2 * c + 2
            shift = (2 * c - slab) % 8
            packed_up = jnp.where(here, pltpu.roll(ups[c], shift, 0) if shift else ups[c], packed_up)
            packed_down = jnp.where(here, pltpu.roll(downs[c], 2 * c + 2, 0), packed_down)
        near.append(jnp.where(odd, packed_down, packed_up))
        far.append(jnp.where(odd, packed_up, packed_down))
    for tiles, ref in ((near, near_ref), (far, far_ref)):
        for t in range(TILES):
            ref[t] = tiles[t]
        ref[TILES] = y_face(tiles, lanes)
        ref[TILES + 1] = z_face(tiles, lanes)
    for c in range(3):
        face_ref[AFTER_Y + c] = y_face(after[c], lanes)
        face_ref[AFTER_Z + c] = z_face(after[c], lanes)
    u1 = [u_ref[1, 0, :, lane(t)] for t in range(TILES)]
    u2 = [u_ref[2, 0, :, lane(t)] for t in range(TILES)]
    face_ref[U1_Y] = y_face(u1, lanes)
    face_ref[U1_Z] = z_face(u1, lanes)
    face_ref[U2_Z] = z_face(u2, lanes)


def last_kernel(slab, slabs, nb_ref, after_ref, u_ref, near_ref, all_ref, out_ref):
    rows, lanes = iotas()
    here = lax.axis_index("blk")
    place_in = lax.axis_index("sub")
    odd = place_in % 2 == 1
    near_row = jnp.where(odd, 0, slab - 2)
    far_row = jnp.where(odd, slab - 2, 0)

    def beside(block, face):
        tile = all_ref[block, FAR]
        only = jnp.where((rows == 6) & (lanes == face), tile, -1.0)
        return jnp.max(only).astype(jnp.int32)

    below_x = place_in == 0
    above_x = place_in == slabs - 1
    x_face = jnp.where(above_x, 1, 0)

    def far_block(block):
        return jnp.where(below_x | above_x, beside(block, x_face), block)

    def placed(tile, c, row):
        moved = pltpu.roll(tile, (row - 2 * c + 8) % 8, 0)
        return jnp.where((rows >= row) & (rows < row + 2), moved, 0.0)

    outer = far_block(here)
    after = [[], [], []]
    for t in range(TILES):
        near, far = near_ref[t], all_ref[outer, FAR + t]
        for c in range(3):
            after[c].append(
                after_ref[c, :, lane(t)] + placed(near, c, near_row) + placed(far, c, far_row)
            )

    ym, yp = nb_ref[0, 2], nb_ref[0, 3]
    zm, zp = nb_ref[0, 4], nb_ref[0, 5]
    from_above = lanes < 64

    def mixed(tile, far=False):
        if far:
            a, b = far_block(yp), far_block(ym)
        else:
            a, b = yp, ym
        return jnp.where(from_above, all_ref[a, tile], all_ref[b, tile])

    near, far = mixed(NEAR_Y), mixed(FAR_Y, True)
    weight = weights(mixed(U1_Y))
    one = jnp.where(from_above, weight[-1], weight[1])
    two = jnp.where(from_above, weight[-2], weight[2])
    y_spill = []
    for c in range(3):
        q = mixed(AFTER_Y + c) + placed(near, c, near_row) + placed(far, c, far_row)
        q1, q2 = q * one, q * two
        edge = jnp.where(lanes < 32, pltpu.roll(q1, 32, 1), pltpu.roll(q1, 96, 1))
        y_spill.append(
            pltpu.roll(q2, 64, 1) + jnp.where((lanes < 32) | (lanes >= 96), edge, 0.0)
        )
    after_y = [[None] * TILES for c in range(3)]
    moved = {}
    for t in range(TILES):
        weight = weights(u_ref[1, 0, :, lane(t)])
        for c in range(3):
            q = after[c][t]
            after_y[c][t] = q * weight[0]
            for k in (-2, -1, 1, 2):
                moved[c, t, k] = pltpu.roll(q * weight[k], (32 * k) % 128, 1)
    for t in range(TILES):
        for c in range(3):
            total = after_y[c][t]
            for k in (1, 2):
                cut = lanes < 32 * k
                other = moved[c, t - 1, k] if t > 0 else 0.0
                total = total + jnp.where(cut, other, moved[c, t, k])
                cut = lanes >= 128 - 32 * k
                other = moved[c, t + 1, -k] if t < TILES - 1 else 0.0
                total = total + jnp.where(cut, other, moved[c, t, -k])
            if t == 0:
                total = total + jnp.where(lanes < 64, y_spill[c], 0.0)
            if t == TILES - 1:
                total = total + jnp.where(lanes >= 64, y_spill[c], 0.0)
            after_y[c][t] = total

    place_z = lanes & 3
    y_cell = lanes >> 2
    from_above = place_z < 2
    upper = y_cell < 16
    zpp, zpm = beside(zp, 3), beside(zp, 2)
    zmp, zmm = beside(zm, 3), beside(zm, 2)
    far_zp, far_zm = far_block(zp), far_block(zm)
    far_zpp, far_zpm = far_block(zpp), far_block(zpm)
    far_zmp, far_zmm = far_block(zmp), far_block(zmm)

    def face(tile, a, b):
        return jnp.where(from_above, all_ref[a, tile], all_ref[b, tile])

    def corner(tile, a, b, c, d):
        return jnp.where(upper, face(tile, a, b), face(tile, c, d))

    near, far = face(NEAR_Z, zp, zm), face(FAR_Z, far_zp, far_zm)
    u1 = face(U1_Z, zp, zm)
    u2 = face(U2_Z, zp, zm)
    corner_near = corner(NEAR_Z, zpp, zmp, zpm, zmm)
    corner_far = corner(FAR_Z, far_zpp, far_zmp, far_zpm, far_zmm)
    corner_u1 = corner(U1_Z, zpp, zmp, zpm, zmm)
    own_weight = weights(u1)
    corner_weight = weights(corner_u1)
    weight = weights(u2)
    one = jnp.where(from_above, weight[-1], weight[1])
    two = jnp.where(from_above, weight[-2], weight[2])
    z_spill = []
    for c in range(3):
        q = face(AFTER_Z + c, zp, zm) + placed(near, c, near_row) + placed(far, c, far_row)
        qc = (
            corner(AFTER_Z + c, zpp, zmp, zpm, zmm)
            + placed(corner_near, c, near_row)
            + placed(corner_far, c, far_row)
        )
        total = q * own_weight[0]
        for k in (-2, -1, 1, 2):
            outside = y_cell >= B - k if k > 0 else y_cell < -k
            source = jnp.where(outside, qc * corner_weight[k], q * own_weight[k])
            total = total + pltpu.roll(source, (4 * k) % 128, 1)
        q1, q2 = total * one, total * two
        spill = jnp.where(from_above, pltpu.roll(q2, 126, 1), pltpu.roll(q2, 2, 1))
        edge = jnp.where(place_z == 0, pltpu.roll(q1, 125, 1), pltpu.roll(q1, 3, 1))
        z_spill.append(spill + jnp.where((place_z == 0) | (place_z == 3), edge, 0.0))

    z_cell = lanes & 31
    at_face = (z_cell < 2) | (z_cell >= 30)
    slot = jnp.where(z_cell < 2, z_cell, jnp.where(z_cell >= 30, z_cell - 28, 0))
    for t in range(TILES):
        weight = weights(u_ref[2, 0, :, lane(t)])
        index = 16 * t + 4 * (lanes >> 5) + slot
        for c in range(3):
            q = after_y[c][t]
            total = q * weight[0]
            for k in (1, 2):
                moved = pltpu.roll(q * weight[k], k, 1)
                total = total + jnp.where(z_cell >= k, moved, 0.0)
                moved = pltpu.roll(q * weight[-k], 128 - k, 1)
                total = total + jnp.where(z_cell < B - k, moved, 0.0)
            spill = jnp.take_along_axis(z_spill[c], index, axis=1)
            out_ref[c, 0, :, lane(t)] = total + jnp.where(at_face, spill, 0.0)


def shards(slabs, vorticity, velocity, gradient, neighbour):
    slab = vorticity.shape[2]
    if slab < 8:
        room = ((0, 0), (0, 0), (0, 8 - slab), (0, 0))
        vorticity, velocity, gradient = (
            jnp.pad(a, room) for a in (vorticity, velocity, gradient)
        )
    vmem = pl.BlockSpec(memory_space=pltpu.VMEM)
    smem = pl.BlockSpec(memory_space=pltpu.SMEM)

    def tiles(count):
        return jax.ShapeDtypeStruct((count, 8, 128), jnp.float32)

    after, faces, near, far = pl.pallas_call(
        functools.partial(first_kernel, slab),
        out_shape=(
            jax.ShapeDtypeStruct((3, 8, B * B), jnp.float32),
            tiles(FACES),
            tiles(TILES + 2),
            tiles(TILES + 2),
        ),
        in_specs=[smem, vmem, vmem, vmem],
        out_specs=(vmem, vmem, vmem, vmem),
    )(neighbour, vorticity, velocity, gradient)
    far = lax.ppermute(
        far,
        "sub",
        [p for i in range(1, slabs, 2) for p in ((i, (i + 1) % slabs), ((i + 1) % slabs, i))],
    )
    near = lax.ppermute(
        near, "sub", [p for i in range(0, slabs, 2) for p in ((i, i + 1), (i + 1, i))]
    )
    sent = jnp.concatenate([faces, near[TILES:], far], axis=0)
    everything = lax.all_gather(sent, "blk")
    room = everything.size * 4 + (8 << 20)
    out = pl.pallas_call(
        functools.partial(last_kernel, slab, slabs),
        out_shape=jax.ShapeDtypeStruct((3, 1, 8, B * B), jnp.float32),
        in_specs=[smem, vmem, vmem, vmem, vmem],
        out_specs=vmem,
        compiler_params=pltpu.CompilerParams(vmem_limit_bytes=room),
    )(neighbour, after, velocity, near, everything)
    return out[:, :, :slab]


def solution(mesh):
    return jax.shard_map(
        functools.partial(shards, mesh.shape["sub"]),
        mesh=mesh,
        in_specs=(
            P(None, "blk", "sub", None),
            P(None, "blk", "sub", None),
            P(None, "blk", "sub", None),
            P("blk", None),
        ),
        out_specs=P(None, "blk", "sub", None),
        check_vma=False,
    )
```

```python
import functools

import jax
import jax.numpy as jnp
from jax import lax
from jax.experimental import pallas as pl
from jax.experimental.pallas import tpu as pltpu
from jax.sharding import PartitionSpec as P

B = 32
TILES = B * B // 128
stretch_step = 0.25

AFTER_Y, AFTER_Z, U1_Y, U1_Z, U2_Z = 0, 3, 6, 7, 8
FACES = 9
NEAR_Y, NEAR_Z = 9, 10
FAR, FAR_Y, FAR_Z = 11, 19, 20
SENT = 21


def iotas():
    return (
        lax.broadcasted_iota(jnp.int32, (8, 128), 0),
        lax.broadcasted_iota(jnp.int32, (8, 128), 1),
    )


def weights(u):
    a = jnp.abs(u)
    rest = 1.0 - a
    centre = 1.0 + a * a * (1.5 * a - 2.5)
    toward = a * (0.5 + a * (2.0 - 1.5 * a))
    away = -0.5 * a * rest * rest
    far = -0.5 * a * a * rest
    up = u >= 0.0
    return {
        0: centre,
        1: jnp.where(up, toward, away),
        -1: jnp.where(up, away, toward),
        2: jnp.where(up, far, 0.0),
        -2: jnp.where(up, 0.0, far),
    }


def lane(tile):
    return pl.ds(128 * tile, 128)


def y_face(tiles, lanes):
    return jnp.where(lanes < 64, tiles[0], tiles[TILES - 1])


def z_face(tiles, lanes):
    m = lanes & 3
    index = 32 * ((lanes >> 2) & 3) + jnp.where(m < 2, m, 28 + m)
    face = None
    for t, tile in enumerate(tiles):
        picked = jnp.take_along_axis(tile, index, axis=1)
        face = picked if face is None else jnp.where((lanes >> 4) == t, picked, face)
    return face


def first_kernel(slab, *refs):
    here, (u_ref, after_ref, face_ref, near_ref, far_ref) = refs[:4], refs[4:9]
    nb_ref, w_ref, g_ref, sems = refs[9:]
    copies = [
        pltpu.make_async_copy(source, target, sems.at[n])
        for n, (source, target) in enumerate(zip(here, (nb_ref, w_ref, u_ref, g_ref)))
    ]
    for copy in copies:
        copy.start()
    for copy in copies:
        copy.wait()
    rows, lanes = iotas()
    odd = lax.axis_index("sub") % 2 == 1
    meta = jnp.zeros((8, 128), jnp.float32)
    for j in range(6):
        meta = jnp.where(lanes == j, nb_ref[0, j].astype(jnp.float32), meta)
    after = [[], [], []]
    near, far = [], []
    for t in range(TILES):
        w = [w_ref[c, 0, :, lane(t)] for c in range(3)]
        weight = weights(u_ref[0, 0, :, lane(t)])
        ups, downs = [], []
        for c in range(3):
            q = w[c] + stretch_step * (
                g_ref[3 * c, 0, :, lane(t)] * w[0]
                + g_ref[3 * c + 1, 0, :, lane(t)] * w[1]
                + g_ref[3 * c + 2, 0, :, lane(t)] * w[2]
            )
            inside, up, down = q * weight[0], 0.0, 0.0
            for k in (1, 2):
                moved = pltpu.roll(q * weight[k], k, 0)
                spilt = rows < k if slab == 8 else rows >= slab
                inside = inside + jnp.where(spilt, 0.0, moved)
                up = up + jnp.where(spilt, moved, 0.0)
                moved = pltpu.roll(q * weight[-k], 8 - k, 0)
                spilt = rows >= 8 - k
                inside = inside + jnp.where(spilt, 0.0, moved)
                down = down + jnp.where(spilt, moved, 0.0)
            after[c].append(inside)
            after_ref[c, :, lane(t)] = inside
            ups.append(up)
            downs.append(down)
        rest = meta if t == 0 else 0.0
        packed_up, packed_down = rest, rest
        for c in (2, 1, 0):
            here = rows < 2 * c + 2
            shift = (2 * c - slab) % 8
            packed_up = jnp.where(here, pltpu.roll(ups[c], shift, 0) if shift else ups[c], packed_up)
            packed_down = jnp.where(here, pltpu.roll(downs[c], 2 * c + 2, 0), packed_down)
        near.append(jnp.where(odd, packed_down, packed_up))
        far.append(jnp.where(odd, packed_up, packed_down))
    for tiles, ref in ((near, near_ref), (far, far_ref)):
        for t in range(TILES):
            ref[t] = tiles[t]
        ref[TILES] = y_face(tiles, lanes)
        ref[TILES + 1] = z_face(tiles, lanes)
    for c in range(3):
        face_ref[AFTER_Y + c] = y_face(after[c], lanes)
        face_ref[AFTER_Z + c] = z_face(after[c], lanes)
    u1 = [u_ref[1, 0, :, lane(t)] for t in range(TILES)]
    u2 = [u_ref[2, 0, :, lane(t)] for t in range(TILES)]
    face_ref[U1_Y] = y_face(u1, lanes)
    face_ref[U1_Z] = z_face(u1, lanes)
    face_ref[U2_Z] = z_face(u2, lanes)


def last_kernel(slab, slabs, relative, after_ref, u_ref, near_ref, *refs):
    block_refs, out_ref = refs[:-1], refs[-1]
    rows, lanes = iotas()
    here = lax.axis_index("blk")
    place_in = lax.axis_index("sub")
    odd = place_in % 2 == 1
    near_row = jnp.where(odd, 0, slab - 2)
    far_row = jnp.where(odd, slab - 2, 0)
    below_x = place_in == 0
    above_x = place_in == slabs - 1
    at_end = below_x | above_x
    x_face = jnp.where(above_x, 1, 0)
    base = here if relative else 0

    def over_blocks(step, carry):
        if relative:
            for slot, ref in enumerate(block_refs):
                carry = step(slot, lambda tile, ref=ref: ref[tile], carry)
            return carry
        (ref,) = block_refs
        return lax.fori_loop(
            0, ref.shape[0], lambda slot, c: step(slot, lambda tile: ref[slot, tile], c), carry
        )

    def placed(tile, c, row):
        moved = pltpu.roll(tile, (row - 2 * c + 8) % 8, 0)
        return jnp.where((rows >= row) & (rows < row + 2), moved, 0.0)

    from_above_y = lanes < 64
    place_z = lanes & 3
    y_cell = lanes >> 2
    from_above_z = place_z < 2
    y_face_id = jnp.where(y_cell < 16, 3, 2)
    x_face_id = jnp.full((8, 128), x_face, jnp.int32)

    def beside(tile, face_id):
        row = jnp.broadcast_to(tile[6:7], (8, 128))
        return jnp.take_along_axis(row, face_id, axis=1).astype(jnp.int32) ^ base

    slot_y = beside(near_ref[0], jnp.where(from_above_y, 3, 2))
    slot_z = beside(near_ref[0], jnp.where(from_above_z, 5, 4))
    outer = jnp.where(at_end, beside(near_ref[0], x_face_id), here ^ base)

    def find_corner(slot, tile_at, found):
        return jnp.where(slot_z == slot, beside(tile_at(FAR), y_face_id), found)

    slot_c = over_blocks(find_corner, slot_z)
    slots = (slot_y, slot_z, slot_c)

    def find_far(slot, tile_at, found):
        there = beside(tile_at(FAR), x_face_id)
        return tuple(
            jnp.where(at_end & (start == slot), there, f) for start, f in zip(slots, found)
        )

    far_y, far_z, far_c = over_blocks(find_far, slots)

    wanted = (
        [(slot_y, t) for t in (AFTER_Y, AFTER_Y + 1, AFTER_Y + 2, U1_Y, NEAR_Y)]
        + [(far_y, FAR_Y)]
        + [(slot_z, t) for t in (AFTER_Z, AFTER_Z + 1, AFTER_Z + 2, U1_Z, U2_Z, NEAR_Z)]
        + [(far_z, FAR_Z)]
        + [(slot_c, t) for t in (AFTER_Z, AFTER_Z + 1, AFTER_Z + 2, U1_Z, NEAR_Z)]
        + [(far_c, FAR_Z)]
        + [(outer, FAR + t) for t in range(TILES)]
    )

    def pick(slot, tile_at, picked):
        return tuple(
            jnp.where(which == slot, tile_at(tile), p) for (which, tile), p in zip(wanted, picked)
        )

    zero = jnp.zeros((8, 128), jnp.float32)
    picked = over_blocks(pick, (zero,) * len(wanted))
    y_after, (y_u1, y_near, y_far) = picked[0:3], picked[3:6]
    z_after, (z_u1, z_u2, z_near, z_far) = picked[6:9], picked[9:13]
    c_after, (c_u1, c_near, c_far) = picked[13:16], picked[16:19]
    far_tiles = picked[19:]

    after = [[], [], []]
    for t in range(TILES):
        near, far = near_ref[t], far_tiles[t]
        for c in range(3):
            after[c].append(
                after_ref[c, :, lane(t)] + placed(near, c, near_row) + placed(far, c, far_row)
            )

    weight = weights(y_u1)
    one = jnp.where(from_above_y, weight[-1], weight[1])
    two = jnp.where(from_above_y, weight[-2], weight[2])
    y_spill = []
    for c in range(3):
        q = y_after[c] + placed(y_near, c, near_row) + placed(y_far, c, far_row)
        q1, q2 = q * one, q * two
        edge = jnp.where(lanes < 32, pltpu.roll(q1, 32, 1), pltpu.roll(q1, 96, 1))
        y_spill.append(
            pltpu.roll(q2, 64, 1) + jnp.where((lanes < 32) | (lanes >= 96), edge, 0.0)
        )
    after_y = [[None] * TILES for c in range(3)]
    moved = {}
    for t in range(TILES):
        weight = weights(u_ref[1, 0, :, lane(t)])
        for c in range(3):
            q = after[c][t]
            after_y[c][t] = q * weight[0]
            for k in (-2, -1, 1, 2):
                moved[c, t, k] = pltpu.roll(q * weight[k], (32 * k) % 128, 1)
    for t in range(TILES):
        for c in range(3):
            total = after_y[c][t]
            for k in (1, 2):
                cut = lanes < 32 * k
                other = moved[c, t - 1, k] if t > 0 else 0.0
                total = total + jnp.where(cut, other, moved[c, t, k])
                cut = lanes >= 128 - 32 * k
                other = moved[c, t + 1, -k] if t < TILES - 1 else 0.0
                total = total + jnp.where(cut, other, moved[c, t, -k])
            if t == 0:
                total = total + jnp.where(lanes < 64, y_spill[c], 0.0)
            if t == TILES - 1:
                total = total + jnp.where(lanes >= 64, y_spill[c], 0.0)
            after_y[c][t] = total

    own_weight = weights(z_u1)
    corner_weight = weights(c_u1)
    weight = weights(z_u2)
    one = jnp.where(from_above_z, weight[-1], weight[1])
    two = jnp.where(from_above_z, weight[-2], weight[2])
    z_spill = []
    for c in range(3):
        q = z_after[c] + placed(z_near, c, near_row) + placed(z_far, c, far_row)
        qc = c_after[c] + placed(c_near, c, near_row) + placed(c_far, c, far_row)
        total = q * own_weight[0]
        for k in (-2, -1, 1, 2):
            outside = y_cell >= B - k if k > 0 else y_cell < -k
            source = jnp.where(outside, qc * corner_weight[k], q * own_weight[k])
            total = total + pltpu.roll(source, (4 * k) % 128, 1)
        q1, q2 = total * one, total * two
        spill = jnp.where(from_above_z, pltpu.roll(q2, 126, 1), pltpu.roll(q2, 2, 1))
        edge = jnp.where(place_z == 0, pltpu.roll(q1, 125, 1), pltpu.roll(q1, 3, 1))
        z_spill.append(spill + jnp.where((place_z == 0) | (place_z == 3), edge, 0.0))

    z_cell = lanes & 31
    at_face = (z_cell < 2) | (z_cell >= 30)
    place = jnp.where(z_cell < 2, z_cell, jnp.where(z_cell >= 30, z_cell - 28, 0))
    for t in range(TILES):
        weight = weights(u_ref[2, 0, :, lane(t)])
        index = 16 * t + 4 * (lanes >> 5) + place
        for c in range(3):
            q = after_y[c][t]
            total = q * weight[0]
            for k in (1, 2):
                shifted = pltpu.roll(q * weight[k], k, 1)
                total = total + jnp.where(z_cell >= k, shifted, 0.0)
                shifted = pltpu.roll(q * weight[-k], 128 - k, 1)
                total = total + jnp.where(z_cell < B - k, shifted, 0.0)
            spill = jnp.take_along_axis(z_spill[c], index, axis=1)
            out_ref[c, 0, :, lane(t)] = total + jnp.where(at_face, spill, 0.0)


def swapped(array, d, blocks):
    return lax.ppermute(array, "blk", [(i, i ^ d) for i in range(blocks)])


def shards(slabs, vorticity, velocity, gradient, neighbour):
    slab = vorticity.shape[2]
    if slab < 8:
        room = ((0, 0), (0, 0), (0, 8 - slab), (0, 0))
        vorticity, velocity, gradient = (
            jnp.pad(a, room) for a in (vorticity, velocity, gradient)
        )
    vmem = pl.BlockSpec(memory_space=pltpu.VMEM)
    hbm = pl.BlockSpec(memory_space=pltpu.HBM)

    def tiles(count):
        return jax.ShapeDtypeStruct((count, 8, 128), jnp.float32)

    velocity, after, faces, near, far = pl.pallas_call(
        functools.partial(first_kernel, slab),
        out_shape=(
            jax.ShapeDtypeStruct(velocity.shape, jnp.float32),
            jax.ShapeDtypeStruct((3, 8, B * B), jnp.float32),
            tiles(FACES),
            tiles(TILES + 2),
            tiles(TILES + 2),
        ),
        in_specs=[hbm] * 4,
        out_specs=(vmem,) * 5,
        scratch_shapes=[
            pltpu.SMEM(neighbour.shape, jnp.int32),
            pltpu.VMEM(vorticity.shape, jnp.float32),
            pltpu.VMEM(gradient.shape, jnp.float32),
            pltpu.SemaphoreType.DMA((4,)),
        ],
        compiler_params=pltpu.CompilerParams(vmem_limit_bytes=16 << 20),
    )(*(pltpu.with_memory_space_constraint(a, pltpu.HBM) for a in (neighbour, vorticity, velocity, gradient)))
    far = lax.ppermute(
        far,
        "sub",
        [p for i in range(1, slabs, 2) for p in ((i, (i + 1) % slabs), ((i + 1) % slabs, i))],
    )
    near = lax.ppermute(
        near, "sub", [p for i in range(0, slabs, 2) for p in ((i, i + 1), (i + 1, i))]
    )
    sent = jnp.concatenate([faces, near[TILES:], far], axis=0)
    blocks = lax.axis_size("blk")
    relative = blocks in (2, 4, 8)
    if relative:
        held = {0: sent}
        for d in range(2, blocks, 2):
            held[d] = swapped(sent, d, blocks)
        for d in range(0, blocks, 2):
            held[d + 1] = swapped(held[d], 1, blocks)
        arrays = [held[d] for d in range(blocks)]
    else:
        arrays = [lax.all_gather(sent, "blk")]
    room = (16 << 20) + (0 if relative else arrays[0].size * 4)
    out = pl.pallas_call(
        functools.partial(last_kernel, slab, slabs, relative),
        out_shape=jax.ShapeDtypeStruct((3, 1, 8, B * B), jnp.float32),
        in_specs=[vmem] * (3 + len(arrays)),
        out_specs=vmem,
        compiler_params=pltpu.CompilerParams(vmem_limit_bytes=room),
    )(after, velocity, near, *arrays)
    return out[:, :, :slab]


def solution(mesh):
    return jax.shard_map(
        functools.partial(shards, mesh.shape["sub"]),
        mesh=mesh,
        in_specs=(
            P(None, "blk", "sub", None),
            P(None, "blk", "sub", None),
            P(None, "blk", "sub", None),
            P("blk", None),
        ),
        out_specs=P(None, "blk", "sub", None),
        check_vma=False,
    )
```

```python
import functools

import jax
import jax.numpy as jnp
from jax import lax
from jax.experimental import pallas as pl
from jax.experimental.pallas import tpu as pltpu
from jax.sharding import PartitionSpec as P

B = 32
TILES = B * B // 128
stretch_step = 0.25

AFTER_Y, AFTER_Z, U1_Y, U1_Z, U2_Z = 0, 3, 6, 7, 8
FACES = 9
SPILLS = 6
KEPT = (0, 1, 2, 5, 6, 7)
PACKED = len(KEPT)
ROW_U1_Y, ROW_U1_Z, ROW_U2_Z, ROW_CORNER, ROW_BESIDE = 0, 2, 4, 6, 7
SENT = 2 * PACKED + 1


def iotas():
    return (
        lax.broadcasted_iota(jnp.int32, (8, 128), 0),
        lax.broadcasted_iota(jnp.int32, (8, 128), 1),
    )


def weights(u):
    a = jnp.abs(u)
    rest = 1.0 - a
    centre = 1.0 + a * a * (1.5 * a - 2.5)
    toward = a * (0.5 + a * (2.0 - 1.5 * a))
    away = -0.5 * a * rest * rest
    far = -0.5 * a * a * rest
    up = u >= 0.0
    return {
        0: centre,
        1: jnp.where(up, toward, away),
        -1: jnp.where(up, away, toward),
        2: jnp.where(up, far, 0.0),
        -2: jnp.where(up, 0.0, far),
    }


def lane(tile):
    return pl.ds(128 * tile, 128)


def gathered(tile, index):
    return jnp.take_along_axis(tile, index, axis=1)


def row_of(tile, row):
    return jnp.broadcast_to(tile[row : row + 1], (8, 128))


def pair_rows(tile, row):
    rows, _ = iotas()
    return jnp.where(rows & 1 == 0, row_of(tile, row), row_of(tile, row + 1))


def y_face(tiles):
    _, lanes = iotas()
    return jnp.where(lanes < 64, tiles[0], tiles[TILES - 1])


def z_of(n):
    return jnp.where(n < 2, n, B - 4 + n)


def z_face(tiles):
    _, lanes = iotas()
    index = 32 * ((lanes >> 2) & 3) + z_of(lanes & 3)
    face = None
    for t, tile in enumerate(tiles):
        if tile is not None:
            picked = gathered(tile, index)
            face = picked if face is None else jnp.where((lanes >> 4) == t, picked, face)
    return face


def y_edges(tile):
    _, lanes = iotas()
    y = lanes >> 2
    n = jnp.where(y < 2, y, jnp.where(y >= B - 2, y - (B - 4), 0))
    return gathered(tile, 32 * n + z_of(lanes & 3))


def pack(tiles):
    rows, _ = iotas()
    packed = []
    for j, t in enumerate(KEPT):
        last = jnp.where(rows == 6, pltpu.roll(tiles[3], 6 - j, 0), pltpu.roll(tiles[4], 7 - j, 0))
        packed.append(jnp.where(rows < 6, tiles[t], last))
    return packed


def unpack(packed):
    rows, _ = iotas()
    tiles = dict(zip(KEPT, packed))
    for t, row in ((3, 6), (4, 7)):
        tiles[t] = packed[0]
        for j, tile in enumerate(packed):
            tiles[t] = jnp.where(rows == j, pltpu.roll(tile, (j - row) % 8, 0), tiles[t])
    return [tiles[t] for t in range(TILES)]


def placed(tile, c, row):
    rows, _ = iotas()
    moved = pltpu.roll(tile, (row - 2 * c + 8) % 8, 0)
    return jnp.where((rows >= row) & (rows < row + 2), moved, 0.0)


def y_spill(fields, u):
    _, lanes = iotas()
    weight = weights(u)
    low = lanes < 64
    one = jnp.where(low, weight[-1], weight[1])
    two = jnp.where(low, weight[-2], weight[2])
    spilt = []
    for q in fields:
        q1, q2 = q * one, q * two
        edge = jnp.where(lanes < 32, pltpu.roll(q1, 32, 1), pltpu.roll(q1, 96, 1))
        edge = jnp.where((lanes < 32) | (lanes >= 96), edge, 0.0)
        spilt.append(pltpu.roll(q2, 64, 1) + edge)
    return spilt


def z_spill(fields, u):
    _, lanes = iotas()
    n = lanes & 3
    weight = weights(u)
    one = jnp.where(n < 2, weight[-1], weight[1])
    two = jnp.where(n < 2, weight[-2], weight[2])
    spilt = []
    for q in fields:
        q1, q2 = q * one, q * two
        edge = jnp.where(n == 0, pltpu.roll(q1, 125, 1), pltpu.roll(q1, 3, 1))
        edge = jnp.where((n == 0) | (n == 3), edge, 0.0)
        spilt.append(jnp.where(n < 2, pltpu.roll(q2, 126, 1), pltpu.roll(q2, 2, 1)) + edge)
    return spilt


def y_pass_of_z_face(q, weight, beside=None, beside_weight=None):
    _, lanes = iotas()
    y = lanes >> 2
    total = q * weight[0]
    for k in (-2, -1, 1, 2):
        outside = y >= B - k if k > 0 else y < -k
        other = 0.0 if beside is None else beside * beside_weight[k]
        total = total + pltpu.roll(jnp.where(outside, other, q * weight[k]), (4 * k) % 128, 1)
    return total


def stretched(w_ref, g_ref, t):
    w = [w_ref[c, 0, :, lane(t)] for c in range(3)]
    return [
        w[c]
        + stretch_step
        * (
            g_ref[3 * c, 0, :, lane(t)] * w[0]
            + g_ref[3 * c + 1, 0, :, lane(t)] * w[1]
            + g_ref[3 * c + 2, 0, :, lane(t)] * w[2]
        )
        for c in range(3)
    ]


def spill_kernel(slab, paired, *refs):
    here, (w_ref, u_ref, g_ref, give_ref, keep_ref, meta_ref) = refs[:4], refs[4:10]
    nb_ref, sems = refs[10:]
    copies = [
        pltpu.make_async_copy(source, target, sems.at[n])
        for n, (source, target) in enumerate(zip(here, (nb_ref, w_ref, u_ref, g_ref)))
    ]
    for copy in copies:
        copy.start()
    for copy in copies:
        copy.wait()
    rows, lanes = iotas()
    odd = lax.axis_index("sub") % 2 == 1
    near, far = [], []
    for t in range(TILES):
        q = stretched(w_ref, g_ref, t)
        u = u_ref[0, 0, :, lane(t)]
        top, bottom = q[2], q[2]
        for c in (2, 1, 0):
            mine = rows < 2 * c + 2
            shift = (2 * c + 2 - slab) % 8
            top = jnp.where(mine, pltpu.roll(q[c], shift, 0) if shift else q[c], top)
            bottom = jnp.where(mine, pltpu.roll(q[c], 2 * c, 0) if c else q[c], bottom)
        weight = weights(pair_rows(u, slab - 2))
        edge = jnp.where(rows & 1 == 0, pltpu.roll(top * weight[1], 7, 0), 0.0)
        up = top * weight[2] + edge
        weight = weights(pair_rows(u, 0))
        edge = jnp.where(rows & 1 == 1, pltpu.roll(bottom * weight[-1], 1, 0), 0.0)
        down = bottom * weight[-2] + edge
        near.append(jnp.where(odd, down, up))
        far.append(jnp.where(odd, up, down))
    second = lax.axis_index("blk") % 2 == 1
    for j, (n, f) in enumerate(zip(pack(near), pack(far))):
        give_ref[j] = jnp.where(second, n, f) if paired else f
        keep_ref[j] = jnp.where(second, f, n) if paired else n
    meta = jnp.zeros((8, 128), jnp.float32)
    for j in range(6):
        meta = jnp.where(lanes == j, nb_ref[0, j].astype(jnp.float32), meta)
    meta_ref[...] = meta


def inside_kernel(slab, w_ref, u_ref, g_ref, after_ref, face_ref):
    rows, lanes = iotas()
    after = [[], [], []]
    for t in range(TILES):
        weight = weights(u_ref[0, 0, :, lane(t)])
        for c, q in enumerate(stretched(w_ref, g_ref, t)):
            inside = q * weight[0]
            for k in (1, 2):
                spilt = rows < k if slab == 8 else rows >= slab
                inside = inside + jnp.where(spilt, 0.0, pltpu.roll(q * weight[k], k, 0))
                spilt = rows >= 8 - k
                inside = inside + jnp.where(spilt, 0.0, pltpu.roll(q * weight[-k], 8 - k, 0))
            after[c].append(inside)
            after_ref[c, :, lane(t)] = inside
    u1 = [u_ref[1, 0, :, lane(t)] for t in range(TILES)]
    u2 = [u_ref[2, 0, :, lane(t)] for t in range(TILES)]
    faces = [y_face(after[c]) for c in range(3)] + [z_face(after[c]) for c in range(3)]
    faces += [y_face(u1), z_face(u1), z_face(u2)]
    for n, face in enumerate(faces):
        face_ref[n] = face


def pair_kernel(keep_ref, got_ref, face_ref, both_ref):
    second = lax.axis_index("blk") % 2 == 1
    for j in range(PACKED):
        both_ref[j] = jnp.where(second, got_ref[j], keep_ref[j])
        both_ref[PACKED + j] = jnp.where(second, keep_ref[j], got_ref[j])


def spills_of(slab, face_ref, packed):
    near_row = jnp.where(lax.axis_index("sub") % 2 == 1, 0, slab - 2)
    near = unpack(packed)
    near_y, near_z = y_face(near), z_face(near)
    in_y = [face_ref[AFTER_Y + c] + placed(near_y, c, near_row) for c in range(3)]
    in_z = [face_ref[AFTER_Z + c] + placed(near_z, c, near_row) for c in range(3)]
    weight = weights(face_ref[U1_Z])
    in_z = [y_pass_of_z_face(q, weight) for q in in_z]
    return y_spill(in_y, face_ref[U1_Y]) + z_spill(in_z, face_ref[U2_Z])


def extra_of(slab, face_ref, meta):
    rows, lanes = iotas()
    far_row = jnp.where(lax.axis_index("sub") % 2 == 1, slab - 2, 0)
    extra = meta
    corner = gathered(face_ref[U2_Z], 4 * z_of((lanes >> 2) & 3) + (lanes & 3))
    corner = jnp.sum(jnp.where(rows == lanes >> 4, corner, 0.0), axis=0, keepdims=True)
    extra = jnp.where(rows < ROW_BESIDE, jnp.broadcast_to(corner, (8, 128)), extra)
    for tile, row in ((U2_Z, ROW_U2_Z), (U1_Z, ROW_U1_Z), (U1_Y, ROW_U1_Y)):
        moved = pltpu.roll(face_ref[tile], (row - far_row + 8) % 8, 0)
        extra = jnp.where(rows < row + 2, moved, extra)
    return extra


def middle_kernel(slab, own_ref, got_ref, spill_ref, meta_ref, sent_ref, own_sent_ref):
    second = lax.axis_index("blk") % 2 == 1
    for p, ref in enumerate((own_ref, got_ref)):
        packed = [spill_ref[PACKED * p + j] for j in range(PACKED)]
        for n, tile in enumerate(spills_of(slab, ref, packed)):
            tile = jnp.where(second, packed[n], tile)
            sent_ref[SPILLS * p + n] = tile
            own_sent_ref[SPILLS * p + n] = tile
            if p == 1:
                own_sent_ref[SENT + n] = packed[n]
    extra = extra_of(slab, own_ref, meta_ref[...])
    sent_ref[2 * PACKED] = extra
    own_sent_ref[2 * PACKED] = extra


def middle_kernel_alone(slab, face_ref, near_ref, far_ref, meta_ref, sent_ref):
    packed = [near_ref[j] for j in range(PACKED)]
    for n, tile in enumerate(spills_of(slab, face_ref, packed)):
        sent_ref[n] = tile
        sent_ref[SPILLS + n] = far_ref[n]
    sent_ref[2 * PACKED] = extra_of(slab, face_ref, meta_ref[...])


def last_kernel(slab, slabs, paired, after_ref, u_ref, spill_ref, *refs):
    block_refs, out_ref = refs[:-1], refs[-1]
    rows, lanes = iotas()
    here = lax.axis_index("blk")
    place_in = lax.axis_index("sub")
    odd = place_in % 2 == 1
    near_row = jnp.where(odd, 0, slab - 2)
    far_row = jnp.where(odd, slab - 2, 0)
    below_x = place_in == 0
    above_x = place_in == slabs - 1
    at_end = below_x | above_x
    x_face = jnp.where(above_x, 1, 0)
    second = here % 2 == 1
    base = here - here % 2 if paired else 0

    def over_blocks(step, carry):
        if not paired:
            (ref,) = block_refs
            return lax.fori_loop(
                0,
                ref.shape[0],
                lambda slot, c: step(
                    slot,
                    lambda n: ref[slot, n],
                    lambda j: ref[slot, SPILLS + j],
                    lambda: ref[slot, 2 * PACKED],
                    c,
                ),
                carry,
            )
        chips = len(block_refs) // 2
        for slot in range(2 * chips):
            held, other = block_refs[slot // 2], block_refs[chips + slot // 2]
            p = slot % 2

            def on_core(core, n, held=held, other=other):
                mine, theirs = held[n], other[n]
                return jnp.where(second, theirs, mine) if core == 0 else jnp.where(second, mine, theirs)

            carry = step(
                slot,
                lambda n, p=p, get=on_core: get(0, SPILLS * p + n),
                lambda j, p=p, get=on_core: get(1, PACKED * p + j),
                lambda p=p, get=on_core: get(p, 2 * PACKED),
                carry,
            )
        return carry

    packed = [spill_ref[j] for j in range(PACKED)]
    if paired:
        other = block_refs[len(block_refs) // 2]
        packed = [jnp.where(second, other[SENT + j], packed[j]) for j in range(PACKED)]
    near = unpack(packed)

    def beside(extra, face):
        index = jnp.full((8, 128), face, jnp.int32)
        return gathered(row_of(extra, ROW_BESIDE), index).astype(jnp.int32) ^ base

    own_extra = block_refs[0][2 * PACKED] if paired else block_refs[0][here, 2 * PACKED]
    ym, yp, zm, zp = (beside(own_extra, face) for face in (2, 3, 4, 5))
    outer = jnp.where(at_end, beside(own_extra, x_face), here ^ base)

    def find_corners(slot, spills, far, extra, found):
        tile = extra()
        below, above = (beside(tile, face) for face in (2, 3))
        at_m, at_p = zm == slot, zp == slot
        mm, mp, pm, pp = found
        return (
            jnp.where(at_m, below, mm),
            jnp.where(at_m, above, mp),
            jnp.where(at_p, below, pm),
            jnp.where(at_p, above, pp),
        )

    zmm, zmp, zpm, zpp = over_blocks(find_corners, (zm, zm, zp, zp))
    near_slots = (ym, yp, zm, zp, zmm, zmp, zpm, zpp)

    def find_far(slot, spills, far, extra, found):
        there = beside(extra(), x_face)
        return tuple(
            jnp.where(at_end & (start == slot), there, f) for start, f in zip(near_slots, found)
        )

    far_ym, far_yp, far_zm, far_zp, far_zmm, far_zmp, far_zpm, far_zpp = over_blocks(
        find_far, near_slots
    )

    y_low = lanes < 64
    n_low = lanes & 3 < 2
    z_cell = lanes & 31
    z_low = z_cell < 16
    corner_low, corner_high = jnp.where(z_low, zpm, zmm), jnp.where(z_low, zpp, zmp)
    wanted_spills = (
        [(jnp.where(y_low, ym, yp), n) for n in (0, 1, 2)]
        + [(jnp.where(n_low, zm, zp), n) for n in (3, 4, 5)]
        + [(jnp.where(y_low, corner_low, corner_high), n) for n in (0, 1, 2)]
    )
    wanted_extra = [
        jnp.where(y_low, yp, ym),
        jnp.where(n_low, zp, zm),
        jnp.where(y_low, corner_high, corner_low),
    ]
    far_z = jnp.where(z_low, far_zp, far_zm)
    wanted_far = (
        [(far_yp, 0), (far_ym, PACKED - 1)]
        + [(jnp.where(z_low, far_zpp, far_zmp), 0)]
        + [(jnp.where(z_low, far_zpm, far_zmm), PACKED - 1)]
        + [(far_z, j) for j in range(PACKED)]
        + [(outer, j) for j in range(PACKED)]
    )

    def pick(slot, spills, far, extra, picked):
        tile = extra()
        found = [(which, spills(n)) for which, n in wanted_spills]
        found += [(which, tile) for which in wanted_extra]
        found += [(which, far(j)) for which, j in wanted_far]
        return tuple(jnp.where(which == slot, t, p) for (which, t), p in zip(found, picked))

    count = len(wanted_spills) + len(wanted_extra) + len(wanted_far)
    picked = list(over_blocks(pick, (jnp.zeros((8, 128), jnp.float32),) * count))
    into_y, into_z, into_corner = picked[0:3], picked[3:6], picked[6:9]
    extra_y, extra_z, extra_c = picked[9:12]
    far_y = jnp.where(y_low, picked[12], picked[13])
    far_c = z_face([picked[14]] + [None] * (TILES - 2) + [picked[15]])
    far_z = z_face(unpack(picked[16 : 16 + PACKED]))
    far_own = unpack(picked[16 + PACKED :])

    (by_far,) = y_spill([far_y], pair_rows(extra_y, ROW_U1_Y))
    into_y = [into_y[c] + placed(by_far, c, far_row) for c in range(3)]

    (by_far,) = z_spill(
        [
            y_pass_of_z_face(
                far_z,
                weights(pair_rows(extra_z, ROW_U1_Z)),
                far_c,
                weights(y_edges(pair_rows(extra_c, ROW_U1_Y))),
            )
        ],
        pair_rows(extra_z, ROW_U2_Z),
    )
    y = lanes >> 2
    at_edge = (y < 2) | (y >= B - 2)
    n = jnp.where(y < 2, y, jnp.where(y >= B - 2, y - (B - 4), 0))
    u2 = gathered(row_of(extra_z, ROW_CORNER), 16 * rows + 4 * n + (lanes & 3))
    by_corner = z_spill([jnp.where(at_edge, y_edges(q), 0.0) for q in into_corner], u2)
    into_z = [into_z[c] + by_corner[c] + placed(by_far, c, far_row) for c in range(3)]

    after_y = [[None] * TILES for c in range(3)]
    moved = {}
    for t in range(TILES):
        weight = weights(u_ref[1, 0, :, lane(t)])
        for c in range(3):
            q = after_ref[c, :, lane(t)] + placed(near[t], c, near_row) + placed(far_own[t], c, far_row)
            after_y[c][t] = q * weight[0]
            for k in (-2, -1, 1, 2):
                moved[c, t, k] = pltpu.roll(q * weight[k], (32 * k) % 128, 1)
    for t in range(TILES):
        for c in range(3):
            total = after_y[c][t]
            for k in (1, 2):
                cut = lanes < 32 * k
                other = moved[c, t - 1, k] if t > 0 else 0.0
                total = total + jnp.where(cut, other, moved[c, t, k])
                cut = lanes >= 128 - 32 * k
                other = moved[c, t + 1, -k] if t < TILES - 1 else 0.0
                total = total + jnp.where(cut, other, moved[c, t, -k])
            if t == 0:
                total = total + jnp.where(y_low, into_y[c], 0.0)
            if t == TILES - 1:
                total = total + jnp.where(y_low, 0.0, into_y[c])
            after_y[c][t] = total

    at_face = (z_cell < 2) | (z_cell >= B - 2)
    place = jnp.where(z_cell < 2, z_cell, jnp.where(z_cell >= B - 2, z_cell - (B - 4), 0))
    for t in range(TILES):
        weight = weights(u_ref[2, 0, :, lane(t)])
        index = 16 * t + 4 * (lanes >> 5) + place
        for c in range(3):
            q = after_y[c][t]
            total = q * weight[0]
            for k in (1, 2):
                shifted = pltpu.roll(q * weight[k], k, 1)
                total = total + jnp.where(z_cell >= k, shifted, 0.0)
                shifted = pltpu.roll(q * weight[-k], 128 - k, 1)
                total = total + jnp.where(z_cell < B - k, shifted, 0.0)
            out_ref[c, 0, :, lane(t)] = total + jnp.where(at_face, gathered(into_z[c], index), 0.0)


def swapped(array, d, blocks):
    return lax.ppermute(array, "blk", [(i, i ^ d) for i in range(blocks)])


def near_slab(s, slabs):
    return s ^ 1


def far_slab(s, slabs):
    return (s + 1 if s % 2 else s - 1) % slabs


def shards(slabs, vorticity, velocity, gradient, neighbour):
    slab = vorticity.shape[2]
    if slab < 8:
        room = ((0, 0), (0, 0), (0, 8 - slab), (0, 0))
        vorticity, velocity, gradient = (
            jnp.pad(a, room) for a in (vorticity, velocity, gradient)
        )
    blocks = lax.axis_size("blk")
    paired = blocks in (2, 4, 8)
    vmem = pl.BlockSpec(memory_space=pltpu.VMEM)
    hbm = pl.BlockSpec(memory_space=pltpu.HBM)
    small = pltpu.CompilerParams(vmem_limit_bytes=16 << 20)

    def shape(*dims):
        return jax.ShapeDtypeStruct(dims, jnp.float32)

    def tiles(count):
        return shape(count, 8, 128)

    def call(kernel, out_shape, *args, params=small):
        return pl.pallas_call(
            kernel,
            out_shape=out_shape,
            in_specs=[vmem] * len(args),
            out_specs=(vmem,) * len(out_shape) if isinstance(out_shape, tuple) else vmem,
            compiler_params=params,
        )(*args)

    inputs = (neighbour, vorticity, velocity, gradient)
    vorticity, velocity, gradient, give, keep, meta = pl.pallas_call(
        functools.partial(spill_kernel, slab, paired),
        out_shape=(
            shape(*vorticity.shape),
            shape(*velocity.shape),
            shape(*gradient.shape),
            tiles(PACKED),
            tiles(PACKED),
            shape(8, 128),
        ),
        in_specs=[hbm] * 4,
        out_specs=(vmem,) * 6,
        scratch_shapes=[
            pltpu.SMEM(neighbour.shape, jnp.int32),
            pltpu.SemaphoreType.DMA((4,)),
        ],
        compiler_params=small,
    )(*(pltpu.with_memory_space_constraint(a, pltpu.HBM) for a in inputs))
    after, faces = call(
        functools.partial(inside_kernel, slab),
        (shape(3, 8, B * B), tiles(FACES)),
        vorticity,
        velocity,
        gradient,
    )
    if paired:
        got = swapped(give, 1, blocks)
        both = call(pair_kernel, tiles(2 * PACKED), keep, got, faces)
        spill = lax.ppermute(
            both,
            ("blk", "sub"),
            [
                (b * slabs + s, b * slabs + (far_slab if b % 2 else near_slab)(s, slabs))
                for b in range(blocks)
                for s in range(slabs)
            ],
        )
        got_faces = swapped(faces, 1, blocks)
        sent, own_sent = call(
            functools.partial(middle_kernel, slab),
            (tiles(SENT), tiles(SENT + PACKED)),
            faces,
            got_faces,
            spill,
            meta,
        )
        held = [sent] + [swapped(sent, d, blocks) for d in range(2, blocks, 2)]
        arrays = held + [swapped(array, 1, blocks) for array in [own_sent] + held[1:]]
    else:
        spill = lax.ppermute(keep, "sub", [(s, near_slab(s, slabs)) for s in range(slabs)])
        far = lax.ppermute(give, "sub", [(s, far_slab(s, slabs)) for s in range(slabs)])
        sent = call(
            functools.partial(middle_kernel_alone, slab), tiles(SENT), faces, spill, far, meta
        )
        arrays = [lax.all_gather(sent, "blk")]
    room = (16 << 20) + (0 if paired else arrays[0].size * 4)
    out = call(
        functools.partial(last_kernel, slab, slabs, paired),
        shape(3, 1, 8, B * B),
        after,
        velocity,
        spill,
        *arrays,
        params=pltpu.CompilerParams(vmem_limit_bytes=room),
    )
    return out[:, :, :slab]


def solution(mesh):
    return jax.shard_map(
        functools.partial(shards, mesh.shape["sub"]),
        mesh=mesh,
        in_specs=(
            P(None, "blk", "sub", None),
            P(None, "blk", "sub", None),
            P(None, "blk", "sub", None),
            P("blk", None),
        ),
        out_specs=P(None, "blk", "sub", None),
        check_vma=False,
    )
```

```python
import functools

import jax
import jax.numpy as jnp
from jax import lax
from jax.experimental import pallas as pl
from jax.experimental.pallas import tpu as pltpu
from jax.sharding import PartitionSpec as P

B = 32
TILES = B * B // 128
stretch_step = 0.25

AFTER_Y, AFTER_Z, U1_Y, U1_Z, U2_Z = 0, 3, 6, 7, 8
FACES = 9
SPILLS = 6
KEPT = (0, 1, 2, 5, 6, 7)
PACKED = len(KEPT)
ROW_U1_Y, ROW_U1_Z, ROW_U2_Z, ROW_CORNER, ROW_BESIDE = 0, 2, 4, 6, 7
SENT = 2 * PACKED + 1


def iotas():
    return (
        lax.broadcasted_iota(jnp.int32, (8, 128), 0),
        lax.broadcasted_iota(jnp.int32, (8, 128), 1),
    )


def weights(u):
    a = jnp.abs(u)
    rest = 1.0 - a
    centre = 1.0 + a * a * (1.5 * a - 2.5)
    toward = a * (0.5 + a * (2.0 - 1.5 * a))
    away = -0.5 * a * rest * rest
    far = -0.5 * a * a * rest
    up = u >= 0.0
    return {
        0: centre,
        1: jnp.where(up, toward, away),
        -1: jnp.where(up, away, toward),
        2: jnp.where(up, far, 0.0),
        -2: jnp.where(up, 0.0, far),
    }


def lane(tile):
    return pl.ds(128 * tile, 128)


def gathered(tile, index):
    return jnp.take_along_axis(tile, index, axis=1)


def row_of(tile, row):
    return jnp.broadcast_to(tile[row : row + 1], (8, 128))


def pair_rows(tile, row):
    rows, _ = iotas()
    return jnp.where(rows & 1 == 0, row_of(tile, row), row_of(tile, row + 1))


def y_face(tiles):
    _, lanes = iotas()
    return jnp.where(lanes < 64, tiles[0], tiles[TILES - 1])


def z_of(n):
    return jnp.where(n < 2, n, B - 4 + n)


def z_face(tiles):
    _, lanes = iotas()
    index = 32 * ((lanes >> 2) & 3) + z_of(lanes & 3)
    face = None
    for t, tile in enumerate(tiles):
        if tile is not None:
            picked = gathered(tile, index)
            face = picked if face is None else jnp.where((lanes >> 4) == t, picked, face)
    return face


def y_edges(tile):
    _, lanes = iotas()
    y = lanes >> 2
    n = jnp.where(y < 2, y, jnp.where(y >= B - 2, y - (B - 4), 0))
    return gathered(tile, 32 * n + z_of(lanes & 3))


def pack(tiles):
    rows, _ = iotas()
    packed = []
    for j, t in enumerate(KEPT):
        last = jnp.where(rows == 6, pltpu.roll(tiles[3], 6 - j, 0), pltpu.roll(tiles[4], 7 - j, 0))
        packed.append(jnp.where(rows < 6, tiles[t], last))
    return packed


def unpack(packed):
    rows, _ = iotas()
    tiles = dict(zip(KEPT, packed))
    for t, row in ((3, 6), (4, 7)):
        tiles[t] = packed[0]
        for j, tile in enumerate(packed):
            tiles[t] = jnp.where(rows == j, pltpu.roll(tile, (j - row) % 8, 0), tiles[t])
    return [tiles[t] for t in range(TILES)]


def placed(tile, c, row):
    rows, _ = iotas()
    moved = pltpu.roll(tile, (row - 2 * c + 8) % 8, 0)
    return jnp.where((rows >= row) & (rows < row + 2), moved, 0.0)


def y_spill(fields, u):
    _, lanes = iotas()
    weight = weights(u)
    low = lanes < 64
    one = jnp.where(low, weight[-1], weight[1])
    two = jnp.where(low, weight[-2], weight[2])
    spilt = []
    for q in fields:
        q1, q2 = q * one, q * two
        edge = jnp.where(lanes < 32, pltpu.roll(q1, 32, 1), pltpu.roll(q1, 96, 1))
        edge = jnp.where((lanes < 32) | (lanes >= 96), edge, 0.0)
        spilt.append(pltpu.roll(q2, 64, 1) + edge)
    return spilt


def z_spill(fields, u):
    _, lanes = iotas()
    n = lanes & 3
    weight = weights(u)
    one = jnp.where(n < 2, weight[-1], weight[1])
    two = jnp.where(n < 2, weight[-2], weight[2])
    spilt = []
    for q in fields:
        q1, q2 = q * one, q * two
        edge = jnp.where(n == 0, pltpu.roll(q1, 125, 1), pltpu.roll(q1, 3, 1))
        edge = jnp.where((n == 0) | (n == 3), edge, 0.0)
        spilt.append(jnp.where(n < 2, pltpu.roll(q2, 126, 1), pltpu.roll(q2, 2, 1)) + edge)
    return spilt


def y_pass_of_z_face(q, weight, beside=None, beside_weight=None):
    _, lanes = iotas()
    y = lanes >> 2
    total = q * weight[0]
    for k in (-2, -1, 1, 2):
        outside = y >= B - k if k > 0 else y < -k
        other = 0.0 if beside is None else beside * beside_weight[k]
        total = total + pltpu.roll(jnp.where(outside, other, q * weight[k]), (4 * k) % 128, 1)
    return total


def stretched(w_ref, g_ref, t):
    w = [w_ref[c, 0, :, lane(t)] for c in range(3)]
    return [
        w[c]
        + stretch_step
        * (
            g_ref[3 * c, 0, :, lane(t)] * w[0]
            + g_ref[3 * c + 1, 0, :, lane(t)] * w[1]
            + g_ref[3 * c + 2, 0, :, lane(t)] * w[2]
        )
        for c in range(3)
    ]


def spill_kernel(slab, paired, *refs):
    here, (w_ref, u_ref, g_ref, give_ref, keep_ref, meta_ref) = refs[:4], refs[4:10]
    nb_ref, sems = refs[10:]
    copies = [
        pltpu.make_async_copy(source, target, sems.at[n])
        for n, (source, target) in enumerate(zip(here, (nb_ref, w_ref, u_ref, g_ref)))
    ]
    for copy in copies:
        copy.start()
    for copy in copies:
        copy.wait()
    rows, lanes = iotas()
    odd = lax.axis_index("sub") % 2 == 1
    near, far = [], []
    for t in range(TILES):
        q = stretched(w_ref, g_ref, t)
        u = u_ref[0, 0, :, lane(t)]
        top, bottom = q[2], q[2]
        for c in (2, 1, 0):
            mine = rows < 2 * c + 2
            shift = (2 * c + 2 - slab) % 8
            top = jnp.where(mine, pltpu.roll(q[c], shift, 0) if shift else q[c], top)
            bottom = jnp.where(mine, pltpu.roll(q[c], 2 * c, 0) if c else q[c], bottom)
        weight = weights(pair_rows(u, slab - 2))
        edge = jnp.where(rows & 1 == 0, pltpu.roll(top * weight[1], 7, 0), 0.0)
        up = top * weight[2] + edge
        weight = weights(pair_rows(u, 0))
        edge = jnp.where(rows & 1 == 1, pltpu.roll(bottom * weight[-1], 1, 0), 0.0)
        down = bottom * weight[-2] + edge
        near.append(jnp.where(odd, down, up))
        far.append(jnp.where(odd, up, down))
    second = lax.axis_index("blk") % 2 == 1
    for j, (n, f) in enumerate(zip(pack(near), pack(far))):
        give_ref[j] = jnp.where(second, n, f) if paired else f
        keep_ref[j] = jnp.where(second, f, n) if paired else n
    meta = jnp.zeros((8, 128), jnp.float32)
    for j in range(6):
        meta = jnp.where(lanes == j, nb_ref[0, j].astype(jnp.float32), meta)
    meta_ref[...] = meta


def inside_kernel(slab, w_ref, u_ref, g_ref, meta_ref, after_ref, face_ref):
    rows, lanes = iotas()
    after = [[], [], []]
    for t in range(TILES):
        weight = weights(u_ref[0, 0, :, lane(t)])
        for c, q in enumerate(stretched(w_ref, g_ref, t)):
            inside = q * weight[0]
            for k in (1, 2):
                spilt = rows < k if slab == 8 else rows >= slab
                inside = inside + jnp.where(spilt, 0.0, pltpu.roll(q * weight[k], k, 0))
                spilt = rows >= 8 - k
                inside = inside + jnp.where(spilt, 0.0, pltpu.roll(q * weight[-k], 8 - k, 0))
            after[c].append(inside)
            after_ref[c, :, lane(t)] = inside
    u1 = [u_ref[1, 0, :, lane(t)] for t in range(TILES)]
    u2 = [u_ref[2, 0, :, lane(t)] for t in range(TILES)]
    faces = [y_face(after[c]) for c in range(3)] + [z_face(after[c]) for c in range(3)]
    faces += [y_face(u1), z_face(u1), z_face(u2)]
    for n, face in enumerate(faces):
        face_ref[n] = face
    face_ref[FACES] = extra_of(slab, faces, meta_ref[...])


def pair_kernel(keep_ref, got_ref, face_ref, both_ref):
    second = lax.axis_index("blk") % 2 == 1
    for j in range(PACKED):
        both_ref[j] = jnp.where(second, got_ref[j], keep_ref[j])
        both_ref[PACKED + j] = jnp.where(second, keep_ref[j], got_ref[j])


def spills_of(slab, face_ref, packed):
    near_row = jnp.where(lax.axis_index("sub") % 2 == 1, 0, slab - 2)
    near = unpack(packed)
    near_y, near_z = y_face(near), z_face(near)
    in_y = [face_ref[AFTER_Y + c] + placed(near_y, c, near_row) for c in range(3)]
    in_z = [face_ref[AFTER_Z + c] + placed(near_z, c, near_row) for c in range(3)]
    weight = weights(face_ref[U1_Z])
    in_z = [y_pass_of_z_face(q, weight) for q in in_z]
    return y_spill(in_y, face_ref[U1_Y]) + z_spill(in_z, face_ref[U2_Z])


def extra_of(slab, face_ref, meta):
    rows, lanes = iotas()
    far_row = jnp.where(lax.axis_index("sub") % 2 == 1, slab - 2, 0)
    extra = meta
    corner = gathered(face_ref[U2_Z], 4 * z_of((lanes >> 2) & 3) + (lanes & 3))
    corner = jnp.sum(jnp.where(rows == lanes >> 4, corner, 0.0), axis=0, keepdims=True)
    extra = jnp.where(rows < ROW_BESIDE, jnp.broadcast_to(corner, (8, 128)), extra)
    for tile, row in ((U2_Z, ROW_U2_Z), (U1_Z, ROW_U1_Z), (U1_Y, ROW_U1_Y)):
        moved = pltpu.roll(face_ref[tile], (row - far_row + 8) % 8, 0)
        extra = jnp.where(rows < row + 2, moved, extra)
    return extra


def middle_kernel(slab, own_ref, got_ref, spill_ref, sent_ref, own_sent_ref):
    second = lax.axis_index("blk") % 2 == 1
    packed = [spill_ref[j] for j in range(2 * PACKED)]

    def put(n, tile):
        sent_ref[n] = tile
        own_sent_ref[n] = tile

    @pl.when(second)
    def _():
        for n, tile in enumerate(packed):
            put(n, tile)

    @pl.when(jnp.logical_not(second))
    def _():
        for p, ref in enumerate((own_ref, got_ref)):
            for n, tile in enumerate(spills_of(slab, ref, packed[PACKED * p : PACKED * (p + 1)])):
                put(SPILLS * p + n, tile)

    for j in range(PACKED):
        own_sent_ref[SENT + j] = packed[PACKED + j]
    put(2 * PACKED, own_ref[FACES])


def middle_kernel_alone(slab, face_ref, near_ref, far_ref, sent_ref):
    packed = [near_ref[j] for j in range(PACKED)]
    for n, tile in enumerate(spills_of(slab, face_ref, packed)):
        sent_ref[n] = tile
        sent_ref[SPILLS + n] = far_ref[n]
    sent_ref[2 * PACKED] = face_ref[FACES]


def last_kernel(slab, slabs, paired, after_ref, u_ref, spill_ref, *refs):
    block_refs, out_ref = refs[:-1], refs[-1]
    rows, lanes = iotas()
    here = lax.axis_index("blk")
    place_in = lax.axis_index("sub")
    odd = place_in % 2 == 1
    near_row = jnp.where(odd, 0, slab - 2)
    far_row = jnp.where(odd, slab - 2, 0)
    below_x = place_in == 0
    above_x = place_in == slabs - 1
    at_end = below_x | above_x
    x_face = jnp.where(above_x, 1, 0)
    second = here % 2 == 1
    base = here - here % 2 if paired else 0

    def over_blocks(step, carry):
        if not paired:
            (ref,) = block_refs
            return lax.fori_loop(
                0,
                ref.shape[0],
                lambda slot, c: step(
                    slot,
                    lambda n: ref[slot, n],
                    lambda j: ref[slot, SPILLS + j],
                    lambda: ref[slot, 2 * PACKED],
                    c,
                ),
                carry,
            )
        chips = len(block_refs) // 2
        for slot in range(2 * chips):
            held, other = block_refs[slot // 2], block_refs[chips + slot // 2]
            p = slot % 2

            def on_core(core, n, held=held, other=other, crossed=slot > 1):
                core = 1 - core if crossed else core
                mine, theirs = held[n], other[n]
                return jnp.where(second, theirs, mine) if core == 0 else jnp.where(second, mine, theirs)

            carry = step(
                slot,
                lambda n, p=p, get=on_core: get(0, SPILLS * p + n),
                lambda j, p=p, get=on_core: get(1, PACKED * p + j),
                lambda p=p, get=on_core: get(p, 2 * PACKED),
                carry,
            )
        return carry

    packed = [spill_ref[j] for j in range(PACKED)]
    if paired:
        other = block_refs[len(block_refs) // 2]
        packed = [jnp.where(second, other[SENT + j], packed[j]) for j in range(PACKED)]
    near = unpack(packed)

    def beside(extra, face):
        index = jnp.full((8, 128), face, jnp.int32)
        return gathered(row_of(extra, ROW_BESIDE), index).astype(jnp.int32) ^ base

    own_extra = block_refs[0][2 * PACKED] if paired else block_refs[0][here, 2 * PACKED]
    ym, yp, zm, zp = (beside(own_extra, face) for face in (2, 3, 4, 5))
    outer = jnp.where(at_end, beside(own_extra, x_face), here ^ base)

    def find_corners(slot, spills, far, extra, found):
        tile = extra()
        below, above = (beside(tile, face) for face in (2, 3))
        at_m, at_p = zm == slot, zp == slot
        mm, mp, pm, pp = found
        return (
            jnp.where(at_m, below, mm),
            jnp.where(at_m, above, mp),
            jnp.where(at_p, below, pm),
            jnp.where(at_p, above, pp),
        )

    zmm, zmp, zpm, zpp = over_blocks(find_corners, (zm, zm, zp, zp))
    near_slots = (ym, yp, zm, zp, zmm, zmp, zpm, zpp)

    def find_far(slot, spills, far, extra, found):
        there = beside(extra(), x_face)
        return tuple(
            jnp.where(at_end & (start == slot), there, f) for start, f in zip(near_slots, found)
        )

    far_ym, far_yp, far_zm, far_zp, far_zmm, far_zmp, far_zpm, far_zpp = over_blocks(
        find_far, near_slots
    )

    y_low = lanes < 64
    n_low = lanes & 3 < 2
    z_cell = lanes & 31
    z_low = z_cell < 16
    corner_low, corner_high = jnp.where(z_low, zpm, zmm), jnp.where(z_low, zpp, zmp)
    wanted_spills = (
        [(jnp.where(y_low, ym, yp), n) for n in (0, 1, 2)]
        + [(jnp.where(n_low, zm, zp), n) for n in (3, 4, 5)]
        + [(jnp.where(y_low, corner_low, corner_high), n) for n in (0, 1, 2)]
    )
    wanted_extra = [
        jnp.where(y_low, yp, ym),
        jnp.where(n_low, zp, zm),
        jnp.where(y_low, corner_high, corner_low),
    ]
    far_z = jnp.where(z_low, far_zp, far_zm)
    wanted_far = (
        [(far_yp, 0), (far_ym, PACKED - 1)]
        + [(jnp.where(z_low, far_zpp, far_zmp), 0)]
        + [(jnp.where(z_low, far_zpm, far_zmm), PACKED - 1)]
        + [(far_z, j) for j in range(PACKED)]
        + [(outer, j) for j in range(PACKED)]
    )

    def pick(slot, spills, far, extra, picked):
        tile = extra()
        found = [(which, spills(n)) for which, n in wanted_spills]
        found += [(which, tile) for which in wanted_extra]
        found += [(which, far(j)) for which, j in wanted_far]
        return tuple(jnp.where(which == slot, t, p) for (which, t), p in zip(found, picked))

    count = len(wanted_spills) + len(wanted_extra) + len(wanted_far)
    picked = list(over_blocks(pick, (jnp.zeros((8, 128), jnp.float32),) * count))
    into_y, into_z, into_corner = picked[0:3], picked[3:6], picked[6:9]
    extra_y, extra_z, extra_c = picked[9:12]
    far_y = jnp.where(y_low, picked[12], picked[13])
    far_c = z_face([picked[14]] + [None] * (TILES - 2) + [picked[15]])
    far_z = z_face(unpack(picked[16 : 16 + PACKED]))
    far_own = unpack(picked[16 + PACKED :])

    (by_far,) = y_spill([far_y], pair_rows(extra_y, ROW_U1_Y))
    into_y = [into_y[c] + placed(by_far, c, far_row) for c in range(3)]

    (by_far,) = z_spill(
        [
            y_pass_of_z_face(
                far_z,
                weights(pair_rows(extra_z, ROW_U1_Z)),
                far_c,
                weights(y_edges(pair_rows(extra_c, ROW_U1_Y))),
            )
        ],
        pair_rows(extra_z, ROW_U2_Z),
    )
    y = lanes >> 2
    at_edge = (y < 2) | (y >= B - 2)
    n = jnp.where(y < 2, y, jnp.where(y >= B - 2, y - (B - 4), 0))
    u2 = gathered(row_of(extra_z, ROW_CORNER), 16 * rows + 4 * n + (lanes & 3))
    by_corner = z_spill([jnp.where(at_edge, y_edges(q), 0.0) for q in into_corner], u2)
    into_z = [into_z[c] + by_corner[c] + placed(by_far, c, far_row) for c in range(3)]

    after_y = [[None] * TILES for c in range(3)]
    moved = {}
    for t in range(TILES):
        weight = weights(u_ref[1, 0, :, lane(t)])
        for c in range(3):
            q = after_ref[c, :, lane(t)] + placed(near[t], c, near_row) + placed(far_own[t], c, far_row)
            after_y[c][t] = q * weight[0]
            for k in (-2, -1, 1, 2):
                moved[c, t, k] = pltpu.roll(q * weight[k], (32 * k) % 128, 1)
    for t in range(TILES):
        for c in range(3):
            total = after_y[c][t]
            for k in (1, 2):
                cut = lanes < 32 * k
                other = moved[c, t - 1, k] if t > 0 else 0.0
                total = total + jnp.where(cut, other, moved[c, t, k])
                cut = lanes >= 128 - 32 * k
                other = moved[c, t + 1, -k] if t < TILES - 1 else 0.0
                total = total + jnp.where(cut, other, moved[c, t, -k])
            if t == 0:
                total = total + jnp.where(y_low, into_y[c], 0.0)
            if t == TILES - 1:
                total = total + jnp.where(y_low, 0.0, into_y[c])
            after_y[c][t] = total

    at_face = (z_cell < 2) | (z_cell >= B - 2)
    place = jnp.where(z_cell < 2, z_cell, jnp.where(z_cell >= B - 2, z_cell - (B - 4), 0))
    for t in range(TILES):
        weight = weights(u_ref[2, 0, :, lane(t)])
        index = 16 * t + 4 * (lanes >> 5) + place
        for c in range(3):
            q = after_y[c][t]
            total = q * weight[0]
            for k in (1, 2):
                shifted = pltpu.roll(q * weight[k], k, 1)
                total = total + jnp.where(z_cell >= k, shifted, 0.0)
                shifted = pltpu.roll(q * weight[-k], 128 - k, 1)
                total = total + jnp.where(z_cell < B - k, shifted, 0.0)
            out_ref[c, 0, :, lane(t)] = total + jnp.where(at_face, gathered(into_z[c], index), 0.0)


def swapped(array, d, blocks):
    return lax.ppermute(array, "blk", [(i, i ^ d) for i in range(blocks)])


def near_slab(s, slabs):
    return s ^ 1


def far_slab(s, slabs):
    return (s + 1 if s % 2 else s - 1) % slabs


def shards(slabs, vorticity, velocity, gradient, neighbour):
    slab = vorticity.shape[2]
    if slab < 8:
        room = ((0, 0), (0, 0), (0, 8 - slab), (0, 0))
        vorticity, velocity, gradient = (
            jnp.pad(a, room) for a in (vorticity, velocity, gradient)
        )
    blocks = lax.axis_size("blk")
    paired = blocks in (2, 4, 8)
    vmem = pl.BlockSpec(memory_space=pltpu.VMEM)
    hbm = pl.BlockSpec(memory_space=pltpu.HBM)
    small = pltpu.CompilerParams(vmem_limit_bytes=16 << 20)

    def shape(*dims):
        return jax.ShapeDtypeStruct(dims, jnp.float32)

    def tiles(count):
        return shape(count, 8, 128)

    def call(kernel, out_shape, *args, params=small):
        return pl.pallas_call(
            kernel,
            out_shape=out_shape,
            in_specs=[vmem] * len(args),
            out_specs=(vmem,) * len(out_shape) if isinstance(out_shape, tuple) else vmem,
            compiler_params=params,
        )(*args)

    inputs = (neighbour, vorticity, velocity, gradient)
    vorticity, velocity, gradient, give, keep, meta = pl.pallas_call(
        functools.partial(spill_kernel, slab, paired),
        out_shape=(
            shape(*vorticity.shape),
            shape(*velocity.shape),
            shape(*gradient.shape),
            tiles(PACKED),
            tiles(PACKED),
            shape(8, 128),
        ),
        in_specs=[hbm] * 4,
        out_specs=(vmem,) * 6,
        scratch_shapes=[
            pltpu.SMEM(neighbour.shape, jnp.int32),
            pltpu.SemaphoreType.DMA((4,)),
        ],
        compiler_params=small,
    )(*(pltpu.with_memory_space_constraint(a, pltpu.HBM) for a in inputs))
    after, faces = call(
        functools.partial(inside_kernel, slab),
        (shape(3, 8, B * B), tiles(FACES + 1)),
        vorticity,
        velocity,
        gradient,
        meta,
    )
    if paired:
        got = swapped(give, 1, blocks)
        both = call(pair_kernel, tiles(2 * PACKED), keep, got, faces)
        spill = lax.ppermute(
            both,
            ("blk", "sub"),
            [
                (b * slabs + s, b * slabs + (far_slab if b % 2 else near_slab)(s, slabs))
                for b in range(blocks)
                for s in range(slabs)
            ],
        )
        got_faces = swapped(faces, 1, blocks)
        sent, own_sent = call(
            functools.partial(middle_kernel, slab),
            (tiles(SENT), tiles(SENT + PACKED)),
            faces,
            got_faces,
            spill,
        )
        held = [sent] + [swapped(sent, d ^ 1, blocks) for d in range(2, blocks, 2)]
        arrays = held + [swapped(array, 1, blocks) for array in [own_sent] + held[1:]]
    else:
        spill = lax.ppermute(keep, "sub", [(s, near_slab(s, slabs)) for s in range(slabs)])
        far = lax.ppermute(give, "sub", [(s, far_slab(s, slabs)) for s in range(slabs)])
        sent = call(
            functools.partial(middle_kernel_alone, slab), tiles(SENT), faces, spill, far
        )
        arrays = [lax.all_gather(sent, "blk")]
    room = (16 << 20) + (0 if paired else arrays[0].size * 4)
    out = call(
        functools.partial(last_kernel, slab, slabs, paired),
        shape(3, 1, 8, B * B),
        after,
        velocity,
        spill,
        *arrays,
        params=pltpu.CompilerParams(vmem_limit_bytes=room),
    )
    return out[:, :, :slab]


def solution(mesh):
    return jax.shard_map(
        functools.partial(shards, mesh.shape["sub"]),
        mesh=mesh,
        in_specs=(
            P(None, "blk", "sub", None),
            P(None, "blk", "sub", None),
            P(None, "blk", "sub", None),
            P("blk", None),
        ),
        out_specs=P(None, "blk", "sub", None),
        check_vma=False,
    )
```

```python
import functools

import jax
import jax.numpy as jnp
from jax import lax
from jax.experimental import pallas as pl
from jax.experimental.pallas import tpu as pltpu
from jax.sharding import PartitionSpec as P

B = 32
TILES = B * B // 128
stretch_step = 0.25

AFTER_Y, AFTER_Z, U1_Y, U1_Z, U2_Z = 0, 3, 6, 7, 8
FACES = 9
EXTRA = FACES
SPILLS = 6
KEPT = (0, 1, 2, 5, 6, 7)
PACKED = len(KEPT)
ROW_U1_Y, ROW_U1_Z, ROW_U2_Z, ROW_CORNER, ROW_BESIDE = 0, 2, 4, 6, 7
SENT = SPILLS + 1 + PACKED


def iotas():
    return (
        lax.broadcasted_iota(jnp.int32, (8, 128), 0),
        lax.broadcasted_iota(jnp.int32, (8, 128), 1),
    )


def weights(u):
    a = jnp.abs(u)
    rest = 1.0 - a
    centre = 1.0 + a * a * (1.5 * a - 2.5)
    toward = a * (0.5 + a * (2.0 - 1.5 * a))
    away = -0.5 * a * rest * rest
    far = -0.5 * a * a * rest
    up = u >= 0.0
    return {
        0: centre,
        1: jnp.where(up, toward, away),
        -1: jnp.where(up, away, toward),
        2: jnp.where(up, far, 0.0),
        -2: jnp.where(up, 0.0, far),
    }


def lane(tile):
    return pl.ds(128 * tile, 128)


def gathered(tile, index):
    return jnp.take_along_axis(tile, index, axis=1)


def row_of(tile, row):
    return jnp.broadcast_to(tile[row : row + 1], (8, 128))


def pair_rows(tile, row):
    rows, _ = iotas()
    return jnp.where(rows & 1 == 0, row_of(tile, row), row_of(tile, row + 1))


def y_face(tiles):
    _, lanes = iotas()
    return jnp.where(lanes < 64, tiles[0], tiles[TILES - 1])


def z_of(n):
    return jnp.where(n < 2, n, B - 4 + n)


def z_face(tiles):
    _, lanes = iotas()
    index = 32 * ((lanes >> 2) & 3) + z_of(lanes & 3)
    face = None
    for t, tile in enumerate(tiles):
        if tile is not None:
            picked = gathered(tile, index)
            face = picked if face is None else jnp.where((lanes >> 4) == t, picked, face)
    return face


def y_edges(tile):
    _, lanes = iotas()
    y = lanes >> 2
    n = jnp.where(y < 2, y, jnp.where(y >= B - 2, y - (B - 4), 0))
    return gathered(tile, 32 * n + z_of(lanes & 3))


def pack(tiles):
    rows, _ = iotas()
    packed = []
    for j, t in enumerate(KEPT):
        last = jnp.where(rows == 6, pltpu.roll(tiles[3], 6 - j, 0), pltpu.roll(tiles[4], 7 - j, 0))
        packed.append(jnp.where(rows < 6, tiles[t], last))
    return packed


def unpack(packed):
    rows, _ = iotas()
    tiles = dict(zip(KEPT, packed))
    for t, row in ((3, 6), (4, 7)):
        tiles[t] = packed[0]
        for j, tile in enumerate(packed):
            tiles[t] = jnp.where(rows == j, pltpu.roll(tile, (j - row) % 8, 0), tiles[t])
    return [tiles[t] for t in range(TILES)]


def placed(tile, c, row):
    rows, _ = iotas()
    moved = pltpu.roll(tile, (row - 2 * c + 8) % 8, 0)
    return jnp.where((rows >= row) & (rows < row + 2), moved, 0.0)


def y_spill(fields, u):
    _, lanes = iotas()
    weight = weights(u)
    low = lanes < 64
    one = jnp.where(low, weight[-1], weight[1])
    two = jnp.where(low, weight[-2], weight[2])
    spilt = []
    for q in fields:
        q1, q2 = q * one, q * two
        edge = jnp.where(lanes < 32, pltpu.roll(q1, 32, 1), pltpu.roll(q1, 96, 1))
        edge = jnp.where((lanes < 32) | (lanes >= 96), edge, 0.0)
        spilt.append(pltpu.roll(q2, 64, 1) + edge)
    return spilt


def z_spill(fields, u):
    _, lanes = iotas()
    n = lanes & 3
    weight = weights(u)
    one = jnp.where(n < 2, weight[-1], weight[1])
    two = jnp.where(n < 2, weight[-2], weight[2])
    spilt = []
    for q in fields:
        q1, q2 = q * one, q * two
        edge = jnp.where(n == 0, pltpu.roll(q1, 125, 1), pltpu.roll(q1, 3, 1))
        edge = jnp.where((n == 0) | (n == 3), edge, 0.0)
        spilt.append(jnp.where(n < 2, pltpu.roll(q2, 126, 1), pltpu.roll(q2, 2, 1)) + edge)
    return spilt


def y_pass_of_z_face(q, weight, beside=None, beside_weight=None):
    _, lanes = iotas()
    y = lanes >> 2
    total = q * weight[0]
    for k in (-2, -1, 1, 2):
        outside = y >= B - k if k > 0 else y < -k
        other = 0.0 if beside is None else beside * beside_weight[k]
        total = total + pltpu.roll(jnp.where(outside, other, q * weight[k]), (4 * k) % 128, 1)
    return total


def stretched(w_ref, g_ref, t):
    w = [w_ref[c, 0, :, lane(t)] for c in range(3)]
    return [
        w[c]
        + stretch_step
        * (
            g_ref[3 * c, 0, :, lane(t)] * w[0]
            + g_ref[3 * c + 1, 0, :, lane(t)] * w[1]
            + g_ref[3 * c + 2, 0, :, lane(t)] * w[2]
        )
        for c in range(3)
    ]


def spill_kernel(slab, *refs):
    here, (w_ref, u_ref, g_ref, up_ref, down_ref, meta_ref) = refs[:4], refs[4:10]
    nb_ref, sems = refs[10:]
    copies = [
        pltpu.make_async_copy(source, target, sems.at[n])
        for n, (source, target) in enumerate(zip(here, (nb_ref, w_ref, u_ref, g_ref)))
    ]
    for copy in copies:
        copy.start()
    for copy in copies:
        copy.wait()
    rows, lanes = iotas()
    ups, downs = [], []
    for t in range(TILES):
        q = stretched(w_ref, g_ref, t)
        u = u_ref[0, 0, :, lane(t)]
        top, bottom = q[2], q[2]
        for c in (2, 1, 0):
            mine = rows < 2 * c + 2
            shift = (2 * c + 2 - slab) % 8
            top = jnp.where(mine, pltpu.roll(q[c], shift, 0) if shift else q[c], top)
            bottom = jnp.where(mine, pltpu.roll(q[c], 2 * c, 0) if c else q[c], bottom)
        weight = weights(pair_rows(u, slab - 2))
        edge = jnp.where(rows & 1 == 0, pltpu.roll(top * weight[1], 7, 0), 0.0)
        ups.append(top * weight[2] + edge)
        weight = weights(pair_rows(u, 0))
        edge = jnp.where(rows & 1 == 1, pltpu.roll(bottom * weight[-1], 1, 0), 0.0)
        downs.append(bottom * weight[-2] + edge)
    for j, (up, down) in enumerate(zip(pack(ups), pack(downs))):
        up_ref[j], down_ref[j] = up, down
    meta = jnp.zeros((8, 128), jnp.float32)
    for j in range(6):
        meta = jnp.where(lanes == j, nb_ref[0, j].astype(jnp.float32), meta)
    meta_ref[...] = meta


def inside_kernel(slab, slabs, w_ref, u_ref, g_ref, meta_ref, after_ref, face_ref):
    rows, lanes = iotas()
    after = [[], [], []]
    for t in range(TILES):
        weight = weights(u_ref[0, 0, :, lane(t)])
        for c, q in enumerate(stretched(w_ref, g_ref, t)):
            inside = q * weight[0]
            for k in (1, 2):
                spilt = rows < k if slab == 8 else rows >= slab
                inside = inside + jnp.where(spilt, 0.0, pltpu.roll(q * weight[k], k, 0))
                spilt = rows >= 8 - k
                inside = inside + jnp.where(spilt, 0.0, pltpu.roll(q * weight[-k], 8 - k, 0))
            after[c].append(inside)
            after_ref[c, :, lane(t)] = inside
    u1 = [u_ref[1, 0, :, lane(t)] for t in range(TILES)]
    u2 = [u_ref[2, 0, :, lane(t)] for t in range(TILES)]
    faces = [y_face(after[c]) for c in range(3)] + [z_face(after[c]) for c in range(3)]
    faces += [y_face(u1), z_face(u1), z_face(u2)]
    faces.append(extra_of(slab, slabs, faces, meta_ref[...]))
    for n, face in enumerate(faces):
        face_ref[n] = face


def extra_of(slab, slabs, faces, meta):
    rows, lanes = iotas()
    far_row = jnp.where(lax.axis_index("sub") == slabs - 1, slab - 2, 0)
    corner = gathered(faces[U2_Z], 4 * z_of((lanes >> 2) & 3) + (lanes & 3))
    corner = jnp.sum(jnp.where(rows == lanes >> 4, corner, 0.0), axis=0, keepdims=True)
    extra = jnp.where(rows < ROW_BESIDE, jnp.broadcast_to(corner, (8, 128)), meta)
    for tile, row in ((U2_Z, ROW_U2_Z), (U1_Z, ROW_U1_Z), (U1_Y, ROW_U1_Y)):
        moved = pltpu.roll(faces[tile], (row - far_row + 8) % 8, 0)
        extra = jnp.where(rows < row + 2, moved, extra)
    return extra


def spills_of(slab, face_ref, up, down):
    up, down = unpack(up), unpack(down)
    up_y, up_z, down_y, down_z = y_face(up), z_face(up), y_face(down), z_face(down)
    in_y, in_z = [], []
    for c in range(3):
        q = face_ref[AFTER_Y + c] + placed(up_y, c, 0) + placed(down_y, c, slab - 2)
        in_y.append(q)
        q = face_ref[AFTER_Z + c] + placed(up_z, c, 0) + placed(down_z, c, slab - 2)
        in_z.append(q)
    weight = weights(face_ref[U1_Z])
    in_z = [y_pass_of_z_face(q, weight) for q in in_z]
    return y_spill(in_y, face_ref[U1_Y]) + z_spill(in_z, face_ref[U2_Z])


def middle_kernel(slab, slabs, face_ref, own_face_ref, up_ref, down_ref, sent_ref, own_sent_ref):
    first, last = lax.axis_index("sub") == 0, lax.axis_index("sub") == slabs - 1
    up, down, far = [], [], []
    for j in range(PACKED):
        up.append(jnp.where(first, 0.0, up_ref[j]))
        down.append(jnp.where(last, 0.0, down_ref[j]))
        far.append(jnp.where(first, up_ref[j], jnp.where(last, down_ref[j], 0.0)))
    sent = spills_of(slab, face_ref, up, down) + [own_face_ref[EXTRA]] + far
    for n, tile in enumerate(sent):
        sent_ref[n] = tile
    for n, tile in enumerate(sent + up + down):
        own_sent_ref[n] = tile


def y_pass(fields, weight):
    _, lanes = iotas()
    results = []
    for tiles in fields:
        moved = {
            (t, k): pltpu.roll(tiles[t] * weight[t][k], (32 * k) % 128, 1)
            for t in range(TILES)
            for k in (-2, -1, 1, 2)
        }
        result = []
        for t in range(TILES):
            total = tiles[t] * weight[t][0]
            for k in (1, 2):
                other = moved[t - 1, k] if t > 0 else 0.0
                total = total + jnp.where(lanes < 32 * k, other, moved[t, k])
                other = moved[t + 1, -k] if t < TILES - 1 else 0.0
                total = total + jnp.where(lanes >= 128 - 32 * k, other, moved[t, -k])
            result.append(total)
        results.append(result)
    return results


def z_pass(q, weight):
    _, lanes = iotas()
    z = lanes & 31
    total = q * weight[0]
    for k in (1, 2):
        total = total + jnp.where(z >= k, pltpu.roll(q * weight[k], k, 1), 0.0)
        total = total + jnp.where(z < B - k, pltpu.roll(q * weight[-k], 128 - k, 1), 0.0)
    return total


def own_kernel(slab, after_ref, u_ref, near_ref, own_ref):
    up = unpack([near_ref[SENT + j] for j in range(PACKED)])
    down = unpack([near_ref[SENT + PACKED + j] for j in range(PACKED)])
    after = [
        [
            after_ref[c, :, lane(t)] + placed(up[t], c, 0) + placed(down[t], c, slab - 2)
            for t in range(TILES)
        ]
        for c in range(3)
    ]
    after = y_pass(after, [weights(u_ref[1, 0, :, lane(t)]) for t in range(TILES)])
    for t in range(TILES):
        weight = weights(u_ref[2, 0, :, lane(t)])
        for c in range(3):
            own_ref[c, :, lane(t)] = z_pass(after[c][t], weight)


def last_kernel(slab, slabs, paired, own_ref, u_ref, *refs):
    block_refs, out_ref = refs[:-1], refs[-1]
    rows, lanes = iotas()
    here = lax.axis_index("blk")
    place_in = lax.axis_index("sub")
    below_x = place_in == 0
    above_x = place_in == slabs - 1
    at_end = below_x | above_x
    far_row = jnp.where(above_x, slab - 2, 0)
    x_face = jnp.where(above_x, 1, 0)
    second = here % 2 == 1
    base = here - here % 2 if paired else 0

    def over_blocks(step, carry):
        if not paired:
            (ref,) = block_refs
            return lax.fori_loop(
                0,
                ref.shape[0],
                lambda slot, c: step(
                    slot,
                    lambda n: ref[slot, n],
                    lambda j: ref[slot, SPILLS + 1 + j],
                    lambda: ref[slot, SPILLS],
                    c,
                ),
                carry,
            )
        for slot in range(2 * chips):
            n, p = slot // 2, slot % 2
            carry = step(
                slot,
                lambda i, n=n, p=p: prepared(n, p, i),
                lambda j, n=n, p=p: prepared(n, p, SPILLS + 1 + j),
                lambda n=n, p=p: prepared(n, p, SPILLS),
                carry,
            )
        return carry

    chips = len(block_refs) // 2

    def prepared(n, p, tile):
        held, other = block_refs[n][tile], block_refs[chips + n][tile]
        held_by_second = (p == 1) == (2 * n not in (2, 4))
        if tile > SPILLS:
            held_by_second = not held_by_second
        return jnp.where(second, held, other) if held_by_second else jnp.where(second, other, held)

    own_extra = block_refs[0][SPILLS] if paired else block_refs[0][here, SPILLS]

    def beside(extra, face):
        index = jnp.full((8, 128), face, jnp.int32)
        return gathered(row_of(extra, ROW_BESIDE), index).astype(jnp.int32) ^ base

    ym, yp, zm, zp = (beside(own_extra, face) for face in (2, 3, 4, 5))
    outer = jnp.where(at_end, beside(own_extra, x_face), here ^ base)

    def find_corners(slot, spills, far, extra, found):
        tile = extra()
        below, above = (beside(tile, face) for face in (2, 3))
        at_m, at_p = zm == slot, zp == slot
        mm, mp, pm, pp = found
        return (
            jnp.where(at_m, below, mm),
            jnp.where(at_m, above, mp),
            jnp.where(at_p, below, pm),
            jnp.where(at_p, above, pp),
        )

    zmm, zmp, zpm, zpp = over_blocks(find_corners, (zm, zm, zp, zp))
    near_slots = (ym, yp, zm, zp, zmm, zmp, zpm, zpp)

    def find_far(slot, spills, far, extra, found):
        there = beside(extra(), x_face)
        return tuple(
            jnp.where(at_end & (start == slot), there, f) for start, f in zip(near_slots, found)
        )

    far_ym, far_yp, far_zm, far_zp, far_zmm, far_zmp, far_zpm, far_zpp = over_blocks(
        find_far, near_slots
    )

    y_low = lanes < 64
    n_low = lanes & 3 < 2
    z_cell = lanes & 31
    z_low = z_cell < 16
    corner_low, corner_high = jnp.where(z_low, zpm, zmm), jnp.where(z_low, zpp, zmp)
    wanted_spills = (
        [(jnp.where(y_low, ym, yp), n) for n in (0, 1, 2)]
        + [(jnp.where(n_low, zm, zp), n) for n in (3, 4, 5)]
        + [(jnp.where(y_low, corner_low, corner_high), n) for n in (0, 1, 2)]
    )
    wanted_extra = [
        jnp.where(y_low, yp, ym),
        jnp.where(n_low, zp, zm),
        jnp.where(y_low, corner_high, corner_low),
    ]
    far_z = jnp.where(z_low, far_zp, far_zm)
    wanted_far = (
        [(far_yp, 0), (far_ym, PACKED - 1)]
        + [(jnp.where(z_low, far_zpp, far_zmp), 0)]
        + [(jnp.where(z_low, far_zpm, far_zmm), PACKED - 1)]
        + [(far_z, j) for j in range(PACKED)]
        + [(outer, j) for j in range(PACKED)]
    )

    def pick(slot, spills, far, extra, picked):
        tile = extra()
        found = [(which, spills(n)) for which, n in wanted_spills]
        found += [(which, tile) for which in wanted_extra]
        found += [(which, far(j)) for which, j in wanted_far]
        return tuple(jnp.where(which == slot, t, p) for (which, t), p in zip(found, picked))

    count = len(wanted_spills) + len(wanted_extra) + len(wanted_far)
    picked = list(over_blocks(pick, (jnp.zeros((8, 128), jnp.float32),) * count))
    into_y, into_z, into_corner = picked[0:3], picked[3:6], picked[6:9]
    extra_y, extra_z, extra_c = picked[9:12]
    far_y = jnp.where(y_low, picked[12], picked[13])
    far_c = z_face([picked[14]] + [None] * (TILES - 2) + [picked[15]])
    far_z = z_face(unpack(picked[16 : 16 + PACKED]))
    far_own = unpack(picked[16 + PACKED :])

    (by_far,) = y_spill([far_y], pair_rows(extra_y, ROW_U1_Y))
    into_y = [into_y[c] + placed(by_far, c, far_row) for c in range(3)]

    (by_far,) = z_spill(
        [
            y_pass_of_z_face(
                far_z,
                weights(pair_rows(extra_z, ROW_U1_Z)),
                far_c,
                weights(y_edges(pair_rows(extra_c, ROW_U1_Y))),
            )
        ],
        pair_rows(extra_z, ROW_U2_Z),
    )
    y = lanes >> 2
    at_edge = (y < 2) | (y >= B - 2)
    n = jnp.where(y < 2, y, jnp.where(y >= B - 2, y - (B - 4), 0))
    u2 = gathered(row_of(extra_z, ROW_CORNER), 16 * rows + 4 * n + (lanes & 3))
    by_corner = z_spill([jnp.where(at_edge, y_edges(q), 0.0) for q in into_corner], u2)
    into_z = [into_z[c] + by_corner[c] + placed(by_far, c, far_row) for c in range(3)]

    def far_rows(c, t):
        u = pltpu.roll(u_ref[c, 0, :, lane(t)], (8 - far_row) % 8, 0)
        return weights(pair_rows(u, 0))

    packed = y_pass([far_own], [far_rows(1, t) for t in range(TILES)])[0]
    packed = [z_pass(packed[t], far_rows(2, t)) for t in range(TILES)]
    u2 = y_face([u_ref[2, 0, :, lane(t)] for t in range(TILES)])
    weight = weights(u2)
    into_y = [z_pass(q, weight) for q in into_y]
    at_face = (z_cell < 2) | (z_cell >= B - 2)
    place = jnp.where(z_cell < 2, z_cell, jnp.where(z_cell >= B - 2, z_cell - (B - 4), 0))
    for t in range(TILES):
        index = 16 * t + 4 * (lanes >> 5) + place
        for c in range(3):
            total = own_ref[c, :, lane(t)] + placed(packed[t], c, far_row)
            if t == 0:
                total = total + jnp.where(y_low, into_y[c], 0.0)
            if t == TILES - 1:
                total = total + jnp.where(y_low, 0.0, into_y[c])
            out_ref[c, 0, :, lane(t)] = total + jnp.where(at_face, gathered(into_z[c], index), 0.0)


def shards(slabs, vorticity, velocity, gradient, neighbour):
    slab = vorticity.shape[2]
    if slab < 8:
        room = ((0, 0), (0, 0), (0, 8 - slab), (0, 0))
        vorticity, velocity, gradient = (
            jnp.pad(a, room) for a in (vorticity, velocity, gradient)
        )
    blocks = lax.axis_size("blk")
    paired = blocks in (2, 4, 8)
    vmem = pl.BlockSpec(memory_space=pltpu.VMEM)
    hbm = pl.BlockSpec(memory_space=pltpu.HBM)
    small = pltpu.CompilerParams(vmem_limit_bytes=16 << 20)

    def shape(*dims):
        return jax.ShapeDtypeStruct(dims, jnp.float32)

    def tiles(count):
        return shape(count, 8, 128)

    def call(kernel, out_shape, *args, params=small):
        return pl.pallas_call(
            kernel,
            out_shape=out_shape,
            in_specs=[vmem] * len(args),
            out_specs=(vmem,) * len(out_shape) if isinstance(out_shape, tuple) else vmem,
            compiler_params=params,
        )(*args)

    inputs = (neighbour, vorticity, velocity, gradient)
    vorticity, velocity, gradient, up, down, meta = pl.pallas_call(
        functools.partial(spill_kernel, slab),
        out_shape=(
            shape(*vorticity.shape),
            shape(*velocity.shape),
            shape(*gradient.shape),
            tiles(PACKED),
            tiles(PACKED),
            shape(8, 128),
        ),
        in_specs=[hbm] * 4,
        out_specs=(vmem,) * 6,
        scratch_shapes=[
            pltpu.SMEM(neighbour.shape, jnp.int32),
            pltpu.SemaphoreType.DMA((4,)),
        ],
        compiler_params=small,
    )(*(pltpu.with_memory_space_constraint(a, pltpu.HBM) for a in inputs))
    after, faces = call(
        functools.partial(inside_kernel, slab, slabs),
        (shape(3, 8, B * B), tiles(FACES + 1)),
        vorticity,
        velocity,
        gradient,
        meta,
    )

    def moved(array, d, step=0):
        pairs = []
        for b in range(blocks):
            for s in range(slabs):
                c = b ^ d ^ (1 if paired and not 0 <= s + step < slabs else 0)
                pairs.append((b * slabs + s, c * slabs + (s + step) % slabs))
        return lax.ppermute(array, ("blk", "sub"), pairs)

    cross = 0
    up = moved(up, cross, 1)
    down = moved(down, cross, -1)
    their_faces = faces
    sent, near = call(
        functools.partial(middle_kernel, slab, slabs),
        (tiles(SENT), tiles(SENT + 2 * PACKED)),
        their_faces,
        faces,
        up,
        down,
    )
    if paired:
        held = [sent] + [moved(sent, d ^ (d in (2, 4))) for d in range(2, blocks, 2)]
        arrays = held + [moved(array, 1) for array in held]
    else:
        arrays = [lax.all_gather(sent, "blk")]
    own = call(
        functools.partial(own_kernel, slab), shape(3, 8, B * B), after, velocity, near
    )
    room = (16 << 20) + (0 if paired else arrays[0].size * 4)
    out = call(
        functools.partial(last_kernel, slab, slabs, paired),
        shape(3, 1, 8, B * B),
        own,
        velocity,
        *arrays,
        params=pltpu.CompilerParams(vmem_limit_bytes=room),
    )
    return out[:, :, :slab]


def solution(mesh):
    return jax.shard_map(
        functools.partial(shards, mesh.shape["sub"]),
        mesh=mesh,
        in_specs=(
            P(None, "blk", "sub", None),
            P(None, "blk", "sub", None),
            P(None, "blk", "sub", None),
            P("blk", None),
        ),
        out_specs=P(None, "blk", "sub", None),
        check_vma=False,
    )
```

```python
import functools

import jax
import jax.numpy as jnp
from jax import lax
from jax.experimental import pallas as pl
from jax.experimental.pallas import tpu as pltpu
from jax.sharding import PartitionSpec as P

B = 32
TILES = B * B // 128
stretch_step = 0.25

AFTER_Y, AFTER_Z, U1_Y, U1_Z, U2_Z = 0, 3, 6, 7, 8
FACES = 9
EXTRA = FACES
SPILLS = 6
KEPT = (0, 1, 2, 5, 6, 7)
PACKED = len(KEPT)
ROW_U1_Y, ROW_U1_Z, ROW_U2_Z, ROW_CORNER, ROW_BESIDE = 0, 2, 4, 6, 7
SENT = SPILLS + 1 + PACKED
CROSSED = (2, 6)


def iotas():
    return (
        lax.broadcasted_iota(jnp.int32, (8, 128), 0),
        lax.broadcasted_iota(jnp.int32, (8, 128), 1),
    )


def weights(u):
    a = jnp.abs(u)
    rest = 1.0 - a
    centre = 1.0 + a * a * (1.5 * a - 2.5)
    toward = a * (0.5 + a * (2.0 - 1.5 * a))
    away = -0.5 * a * rest * rest
    far = -0.5 * a * a * rest
    up = u >= 0.0
    return {
        0: centre,
        1: jnp.where(up, toward, away),
        -1: jnp.where(up, away, toward),
        2: jnp.where(up, far, 0.0),
        -2: jnp.where(up, 0.0, far),
    }


def lane(tile):
    return pl.ds(128 * tile, 128)


def gathered(tile, index):
    return jnp.take_along_axis(tile, index, axis=1)


def row_of(tile, row):
    return jnp.broadcast_to(tile[row : row + 1], (8, 128))


def pair_rows(tile, row):
    rows, _ = iotas()
    return jnp.where(rows & 1 == 0, row_of(tile, row), row_of(tile, row + 1))


def y_face(tiles):
    _, lanes = iotas()
    return jnp.where(lanes < 64, tiles[0], tiles[TILES - 1])


def z_of(n):
    return jnp.where(n < 2, n, B - 4 + n)


def z_face(tiles):
    _, lanes = iotas()
    index = 32 * ((lanes >> 2) & 3) + z_of(lanes & 3)
    face = None
    for t, tile in enumerate(tiles):
        if tile is not None:
            picked = gathered(tile, index)
            face = picked if face is None else jnp.where((lanes >> 4) == t, picked, face)
    return face


def y_edges(tile):
    _, lanes = iotas()
    y = lanes >> 2
    n = jnp.where(y < 2, y, jnp.where(y >= B - 2, y - (B - 4), 0))
    return gathered(tile, 32 * n + z_of(lanes & 3))


def pack(tiles):
    rows, _ = iotas()
    packed = []
    for j, t in enumerate(KEPT):
        last = jnp.where(rows == 6, pltpu.roll(tiles[3], 6 - j, 0), pltpu.roll(tiles[4], 7 - j, 0))
        packed.append(jnp.where(rows < 6, tiles[t], last))
    return packed


def unpack(packed):
    rows, _ = iotas()
    tiles = dict(zip(KEPT, packed))
    for t, row in ((3, 6), (4, 7)):
        tiles[t] = packed[0]
        for j, tile in enumerate(packed):
            tiles[t] = jnp.where(rows == j, pltpu.roll(tile, (j - row) % 8, 0), tiles[t])
    return [tiles[t] for t in range(TILES)]


def placed(tile, c, row):
    rows, _ = iotas()
    moved = pltpu.roll(tile, (row - 2 * c + 8) % 8, 0)
    return jnp.where((rows >= row) & (rows < row + 2), moved, 0.0)


def y_spill(fields, u):
    _, lanes = iotas()
    weight = weights(u)
    low = lanes < 64
    one = jnp.where(low, weight[-1], weight[1])
    two = jnp.where(low, weight[-2], weight[2])
    spilt = []
    for q in fields:
        q1, q2 = q * one, q * two
        edge = jnp.where(lanes < 32, pltpu.roll(q1, 32, 1), pltpu.roll(q1, 96, 1))
        edge = jnp.where((lanes < 32) | (lanes >= 96), edge, 0.0)
        spilt.append(pltpu.roll(q2, 64, 1) + edge)
    return spilt


def z_spill(fields, u):
    _, lanes = iotas()
    n = lanes & 3
    weight = weights(u)
    one = jnp.where(n < 2, weight[-1], weight[1])
    two = jnp.where(n < 2, weight[-2], weight[2])
    spilt = []
    for q in fields:
        q1, q2 = q * one, q * two
        edge = jnp.where(n == 0, pltpu.roll(q1, 125, 1), pltpu.roll(q1, 3, 1))
        edge = jnp.where((n == 0) | (n == 3), edge, 0.0)
        spilt.append(jnp.where(n < 2, pltpu.roll(q2, 126, 1), pltpu.roll(q2, 2, 1)) + edge)
    return spilt


def y_pass_of_z_face(q, weight, beside=None, beside_weight=None):
    _, lanes = iotas()
    y = lanes >> 2
    total = q * weight[0]
    for k in (-2, -1, 1, 2):
        outside = y >= B - k if k > 0 else y < -k
        other = 0.0 if beside is None else beside * beside_weight[k]
        total = total + pltpu.roll(jnp.where(outside, other, q * weight[k]), (4 * k) % 128, 1)
    return total


def stretched(w_ref, g_ref, t):
    w = [w_ref[c, 0, :, lane(t)] for c in range(3)]
    return [
        w[c]
        + stretch_step
        * (
            g_ref[3 * c, 0, :, lane(t)] * w[0]
            + g_ref[3 * c + 1, 0, :, lane(t)] * w[1]
            + g_ref[3 * c + 2, 0, :, lane(t)] * w[2]
        )
        for c in range(3)
    ]


def spill_kernel(slab, *refs):
    here, (w_ref, u_ref, g_ref, up_ref, down_ref, meta_ref) = refs[:4], refs[4:10]
    nb_ref, sems = refs[10:]
    copies = [
        pltpu.make_async_copy(source, target, sems.at[n])
        for n, (source, target) in enumerate(zip(here, (nb_ref, w_ref, u_ref, g_ref)))
    ]
    for copy in copies:
        copy.start()
    for copy in copies:
        copy.wait()
    rows, lanes = iotas()
    ups, downs = [], []
    for t in range(TILES):
        q = stretched(w_ref, g_ref, t)
        u = u_ref[0, 0, :, lane(t)]
        top, bottom = q[2], q[2]
        for c in (2, 1, 0):
            mine = rows < 2 * c + 2
            shift = (2 * c + 2 - slab) % 8
            top = jnp.where(mine, pltpu.roll(q[c], shift, 0) if shift else q[c], top)
            bottom = jnp.where(mine, pltpu.roll(q[c], 2 * c, 0) if c else q[c], bottom)
        weight = weights(pair_rows(u, slab - 2))
        edge = jnp.where(rows & 1 == 0, pltpu.roll(top * weight[1], 7, 0), 0.0)
        ups.append(top * weight[2] + edge)
        weight = weights(pair_rows(u, 0))
        edge = jnp.where(rows & 1 == 1, pltpu.roll(bottom * weight[-1], 1, 0), 0.0)
        downs.append(bottom * weight[-2] + edge)
    for j, (up, down) in enumerate(zip(pack(ups), pack(downs))):
        up_ref[j], down_ref[j] = up, down
    meta = jnp.zeros((8, 128), jnp.float32)
    for j in range(6):
        meta = jnp.where(lanes == j, nb_ref[0, j].astype(jnp.float32), meta)
    meta_ref[...] = meta


def inside_kernel(slab, slabs, w_ref, u_ref, g_ref, meta_ref, after_ref, face_ref):
    rows, lanes = iotas()
    after = [[], [], []]
    for t in range(TILES):
        weight = weights(u_ref[0, 0, :, lane(t)])
        for c, q in enumerate(stretched(w_ref, g_ref, t)):
            inside = q * weight[0]
            for k in (1, 2):
                spilt = rows < k if slab == 8 else rows >= slab
                inside = inside + jnp.where(spilt, 0.0, pltpu.roll(q * weight[k], k, 0))
                spilt = rows >= 8 - k
                inside = inside + jnp.where(spilt, 0.0, pltpu.roll(q * weight[-k], 8 - k, 0))
            after[c].append(inside)
            after_ref[c, :, lane(t)] = inside
    u1 = [u_ref[1, 0, :, lane(t)] for t in range(TILES)]
    u2 = [u_ref[2, 0, :, lane(t)] for t in range(TILES)]
    faces = [y_face(after[c]) for c in range(3)] + [z_face(after[c]) for c in range(3)]
    faces += [y_face(u1), z_face(u1), z_face(u2)]
    faces.append(extra_of(slab, slabs, faces, meta_ref[...]))
    for n, face in enumerate(faces):
        face_ref[n] = face


def extra_of(slab, slabs, faces, meta):
    rows, lanes = iotas()
    far_row = jnp.where(lax.axis_index("sub") == slabs - 1, slab - 2, 0)
    corner = gathered(faces[U2_Z], 4 * z_of((lanes >> 2) & 3) + (lanes & 3))
    corner = jnp.sum(jnp.where(rows == lanes >> 4, corner, 0.0), axis=0, keepdims=True)
    extra = jnp.where(rows < ROW_BESIDE, jnp.broadcast_to(corner, (8, 128)), meta)
    for tile, row in ((U2_Z, ROW_U2_Z), (U1_Z, ROW_U1_Z), (U1_Y, ROW_U1_Y)):
        moved = pltpu.roll(faces[tile], (row - far_row + 8) % 8, 0)
        extra = jnp.where(rows < row + 2, moved, extra)
    return extra


def spills_of(slab, face_ref, up, down):
    up, down = unpack(up), unpack(down)
    up_y, up_z, down_y, down_z = y_face(up), z_face(up), y_face(down), z_face(down)
    in_y, in_z = [], []
    for c in range(3):
        q = face_ref[AFTER_Y + c] + placed(up_y, c, 0) + placed(down_y, c, slab - 2)
        in_y.append(q)
        q = face_ref[AFTER_Z + c] + placed(up_z, c, 0) + placed(down_z, c, slab - 2)
        in_z.append(q)
    weight = weights(face_ref[U1_Z])
    in_z = [y_pass_of_z_face(q, weight) for q in in_z]
    return y_spill(in_y, face_ref[U1_Y]) + z_spill(in_z, face_ref[U2_Z])


def middle_kernel(slab, slabs, face_ref, own_face_ref, up_ref, down_ref, sent_ref, own_sent_ref):
    first, last = lax.axis_index("sub") == 0, lax.axis_index("sub") == slabs - 1
    up, down, far = [], [], []
    for j in range(PACKED):
        up.append(jnp.where(first, 0.0, up_ref[j]))
        down.append(jnp.where(last, 0.0, down_ref[j]))
        far.append(jnp.where(first, up_ref[j], jnp.where(last, down_ref[j], 0.0)))
    sent = spills_of(slab, face_ref, up, down) + [own_face_ref[EXTRA]] + far
    for n, tile in enumerate(sent):
        sent_ref[n] = tile
    for n, tile in enumerate(sent + up + down):
        own_sent_ref[n] = tile


def y_pass(fields, weight):
    _, lanes = iotas()
    results = []
    for tiles in fields:
        moved = {
            (t, k): pltpu.roll(tiles[t] * weight[t][k], (32 * k) % 128, 1)
            for t in range(TILES)
            for k in (-2, -1, 1, 2)
        }
        result = []
        for t in range(TILES):
            total = tiles[t] * weight[t][0]
            for k in (1, 2):
                other = moved[t - 1, k] if t > 0 else 0.0
                total = total + jnp.where(lanes < 32 * k, other, moved[t, k])
                other = moved[t + 1, -k] if t < TILES - 1 else 0.0
                total = total + jnp.where(lanes >= 128 - 32 * k, other, moved[t, -k])
            result.append(total)
        results.append(result)
    return results


def z_pass(q, weight):
    _, lanes = iotas()
    z = lanes & 31
    total = q * weight[0]
    for k in (1, 2):
        total = total + jnp.where(z >= k, pltpu.roll(q * weight[k], k, 1), 0.0)
        total = total + jnp.where(z < B - k, pltpu.roll(q * weight[-k], 128 - k, 1), 0.0)
    return total


def own_kernel(slab, after_ref, u_ref, near_ref, own_ref):
    up = unpack([near_ref[SENT + j] for j in range(PACKED)])
    down = unpack([near_ref[SENT + PACKED + j] for j in range(PACKED)])
    after = [
        [
            after_ref[c, :, lane(t)] + placed(up[t], c, 0) + placed(down[t], c, slab - 2)
            for t in range(TILES)
        ]
        for c in range(3)
    ]
    after = y_pass(after, [weights(u_ref[1, 0, :, lane(t)]) for t in range(TILES)])
    for t in range(TILES):
        weight = weights(u_ref[2, 0, :, lane(t)])
        for c in range(3):
            own_ref[c, :, lane(t)] = z_pass(after[c][t], weight)


def last_kernel(slab, slabs, paired, own_ref, u_ref, *refs):
    block_refs, out_ref = refs[:-1], refs[-1]
    rows, lanes = iotas()
    here = lax.axis_index("blk")
    place_in = lax.axis_index("sub")
    below_x = place_in == 0
    above_x = place_in == slabs - 1
    at_end = below_x | above_x
    far_row = jnp.where(above_x, slab - 2, 0)
    x_face = jnp.where(above_x, 1, 0)
    second = here % 2 == 1
    base = here - here % 2 if paired else 0

    def over_blocks(step, carry):
        if not paired:
            (ref,) = block_refs
            return lax.fori_loop(
                0,
                ref.shape[0],
                lambda slot, c: step(
                    slot,
                    lambda n: ref[slot, n],
                    lambda j: ref[slot, SPILLS + 1 + j],
                    lambda: ref[slot, SPILLS],
                    c,
                ),
                carry,
            )
        for slot in range(2 * chips):
            n, p = slot // 2, slot % 2
            carry = step(
                slot,
                lambda i, n=n, p=p: prepared(n, p, i),
                lambda j, n=n, p=p: prepared(n, p, SPILLS + 1 + j),
                lambda n=n, p=p: prepared(n, p, SPILLS),
                carry,
            )
        return carry

    chips = len(block_refs) // 2

    def prepared(n, p, tile):
        held, other = block_refs[n][tile], block_refs[chips + n][tile]
        held_by_second = (p == 1) == (2 * n not in CROSSED)
        return jnp.where(second, held, other) if held_by_second else jnp.where(second, other, held)

    own_extra = block_refs[0][SPILLS] if paired else block_refs[0][here, SPILLS]

    def beside(extra, face):
        index = jnp.full((8, 128), face, jnp.int32)
        return gathered(row_of(extra, ROW_BESIDE), index).astype(jnp.int32) ^ base

    ym, yp, zm, zp = (beside(own_extra, face) for face in (2, 3, 4, 5))
    outer = jnp.where(at_end, beside(own_extra, x_face), here ^ base)

    def find_corners(slot, spills, far, extra, found):
        tile = extra()
        below, above = (beside(tile, face) for face in (2, 3))
        at_m, at_p = zm == slot, zp == slot
        mm, mp, pm, pp = found
        return (
            jnp.where(at_m, below, mm),
            jnp.where(at_m, above, mp),
            jnp.where(at_p, below, pm),
            jnp.where(at_p, above, pp),
        )

    zmm, zmp, zpm, zpp = over_blocks(find_corners, (zm, zm, zp, zp))
    near_slots = (ym, yp, zm, zp, zmm, zmp, zpm, zpp)

    def find_far(slot, spills, far, extra, found):
        there = beside(extra(), x_face)
        return tuple(
            jnp.where(at_end & (start == slot), there, f) for start, f in zip(near_slots, found)
        )

    far_ym, far_yp, far_zm, far_zp, far_zmm, far_zmp, far_zpm, far_zpp = over_blocks(
        find_far, near_slots
    )

    y_low = lanes < 64
    n_low = lanes & 3 < 2
    z_cell = lanes & 31
    z_low = z_cell < 16
    corner_low, corner_high = jnp.where(z_low, zpm, zmm), jnp.where(z_low, zpp, zmp)
    wanted_spills = (
        [(jnp.where(y_low, ym, yp), n) for n in (0, 1, 2)]
        + [(jnp.where(n_low, zm, zp), n) for n in (3, 4, 5)]
        + [(jnp.where(y_low, corner_low, corner_high), n) for n in (0, 1, 2)]
    )
    wanted_extra = [
        jnp.where(y_low, yp, ym),
        jnp.where(n_low, zp, zm),
        jnp.where(y_low, corner_high, corner_low),
    ]
    far_z = jnp.where(z_low, far_zp, far_zm)
    wanted_far = (
        [(far_yp, 0), (far_ym, PACKED - 1)]
        + [(jnp.where(z_low, far_zpp, far_zmp), 0)]
        + [(jnp.where(z_low, far_zpm, far_zmm), PACKED - 1)]
        + [(far_z, j) for j in range(PACKED)]
        + [(outer, j) for j in range(PACKED)]
    )

    def pick(slot, spills, far, extra, picked):
        tile = extra()
        found = [(which, spills(n)) for which, n in wanted_spills]
        found += [(which, tile) for which in wanted_extra]
        found += [(which, far(j)) for which, j in wanted_far]
        return tuple(jnp.where(which == slot, t, p) for (which, t), p in zip(found, picked))

    count = len(wanted_spills) + len(wanted_extra) + len(wanted_far)
    picked = list(over_blocks(pick, (jnp.zeros((8, 128), jnp.float32),) * count))
    into_y, into_z, into_corner = picked[0:3], picked[3:6], picked[6:9]
    extra_y, extra_z, extra_c = picked[9:12]
    far_y = jnp.where(y_low, picked[12], picked[13])
    far_c = z_face([picked[14]] + [None] * (TILES - 2) + [picked[15]])
    far_z = z_face(unpack(picked[16 : 16 + PACKED]))
    far_own = unpack(picked[16 + PACKED :])

    (by_far,) = y_spill([far_y], pair_rows(extra_y, ROW_U1_Y))
    into_y = [into_y[c] + placed(by_far, c, far_row) for c in range(3)]

    (by_far,) = z_spill(
        [
            y_pass_of_z_face(
                far_z,
                weights(pair_rows(extra_z, ROW_U1_Z)),
                far_c,
                weights(y_edges(pair_rows(extra_c, ROW_U1_Y))),
            )
        ],
        pair_rows(extra_z, ROW_U2_Z),
    )
    y = lanes >> 2
    at_edge = (y < 2) | (y >= B - 2)
    n = jnp.where(y < 2, y, jnp.where(y >= B - 2, y - (B - 4), 0))
    u2 = gathered(row_of(extra_z, ROW_CORNER), 16 * rows + 4 * n + (lanes & 3))
    by_corner = z_spill([jnp.where(at_edge, y_edges(q), 0.0) for q in into_corner], u2)
    into_z = [into_z[c] + by_corner[c] + placed(by_far, c, far_row) for c in range(3)]

    def far_rows(c, t):
        u = pltpu.roll(u_ref[c, 0, :, lane(t)], (8 - far_row) % 8, 0)
        return weights(pair_rows(u, 0))

    packed = y_pass([far_own], [far_rows(1, t) for t in range(TILES)])[0]
    packed = [z_pass(packed[t], far_rows(2, t)) for t in range(TILES)]
    u2 = y_face([u_ref[2, 0, :, lane(t)] for t in range(TILES)])
    weight = weights(u2)
    into_y = [z_pass(q, weight) for q in into_y]
    at_face = (z_cell < 2) | (z_cell >= B - 2)
    place = jnp.where(z_cell < 2, z_cell, jnp.where(z_cell >= B - 2, z_cell - (B - 4), 0))
    for t in range(TILES):
        index = 16 * t + 4 * (lanes >> 5) + place
        for c in range(3):
            total = own_ref[c, :, lane(t)] + placed(packed[t], c, far_row)
            if t == 0:
                total = total + jnp.where(y_low, into_y[c], 0.0)
            if t == TILES - 1:
                total = total + jnp.where(y_low, 0.0, into_y[c])
            out_ref[c, 0, :, lane(t)] = total + jnp.where(at_face, gathered(into_z[c], index), 0.0)


def shards(slabs, vorticity, velocity, gradient, neighbour):
    slab = vorticity.shape[2]
    if slab < 8:
        room = ((0, 0), (0, 0), (0, 8 - slab), (0, 0))
        vorticity, velocity, gradient = (
            jnp.pad(a, room) for a in (vorticity, velocity, gradient)
        )
    blocks = lax.axis_size("blk")
    paired = blocks in (2, 4, 8)
    vmem = pl.BlockSpec(memory_space=pltpu.VMEM)
    hbm = pl.BlockSpec(memory_space=pltpu.HBM)
    small = pltpu.CompilerParams(vmem_limit_bytes=16 << 20)

    def shape(*dims):
        return jax.ShapeDtypeStruct(dims, jnp.float32)

    def tiles(count):
        return shape(count, 8, 128)

    def call(kernel, out_shape, *args, params=small):
        return pl.pallas_call(
            kernel,
            out_shape=out_shape,
            in_specs=[vmem] * len(args),
            out_specs=(vmem,) * len(out_shape) if isinstance(out_shape, tuple) else vmem,
            compiler_params=params,
        )(*args)

    inputs = (neighbour, vorticity, velocity, gradient)
    vorticity, velocity, gradient, up, down, meta = pl.pallas_call(
        functools.partial(spill_kernel, slab),
        out_shape=(
            shape(*vorticity.shape),
            shape(*velocity.shape),
            shape(*gradient.shape),
            tiles(PACKED),
            tiles(PACKED),
            shape(8, 128),
        ),
        in_specs=[hbm] * 4,
        out_specs=(vmem,) * 6,
        scratch_shapes=[
            pltpu.SMEM(neighbour.shape, jnp.int32),
            pltpu.SemaphoreType.DMA((4,)),
        ],
        compiler_params=small,
    )(*(pltpu.with_memory_space_constraint(a, pltpu.HBM) for a in inputs))
    after, faces = call(
        functools.partial(inside_kernel, slab, slabs),
        (shape(3, 8, B * B), tiles(FACES + 1)),
        vorticity,
        velocity,
        gradient,
        meta,
    )

    def moved(array, d, step=0):
        pairs = []
        for b in range(blocks):
            for s in range(slabs):
                c = b ^ d
                pairs.append((b * slabs + s, c * slabs + (s + step) % slabs))
        return lax.ppermute(array, ("blk", "sub"), pairs)

    cross = 0
    up = moved(up, cross, 1)
    down = moved(down, cross, -1)
    their_faces = faces
    sent, near = call(
        functools.partial(middle_kernel, slab, slabs),
        (tiles(SENT), tiles(SENT + 2 * PACKED)),
        their_faces,
        faces,
        up,
        down,
    )
    if paired:
        held, theirs = [sent], [moved(sent, 1)]
        for d in range(2, blocks, 2):
            held.append(moved(sent, d ^ (d in CROSSED)))
            theirs.append(moved(sent, d ^ (d not in CROSSED)) if d == 2 else moved(held[-1], 1))
        arrays = held + theirs
    else:
        arrays = [lax.all_gather(sent, "blk")]
    own = call(
        functools.partial(own_kernel, slab), shape(3, 8, B * B), after, velocity, near
    )
    room = (16 << 20) + (0 if paired else arrays[0].size * 4)
    out = call(
        functools.partial(last_kernel, slab, slabs, paired),
        shape(3, 1, 8, B * B),
        own,
        velocity,
        *arrays,
        params=pltpu.CompilerParams(vmem_limit_bytes=room),
    )
    return out[:, :, :slab]


def solution(mesh):
    return jax.shard_map(
        functools.partial(shards, mesh.shape["sub"]),
        mesh=mesh,
        in_specs=(
            P(None, "blk", "sub", None),
            P(None, "blk", "sub", None),
            P(None, "blk", "sub", None),
            P("blk", None),
        ),
        out_specs=P(None, "blk", "sub", None),
        check_vma=False,
    )
```

```python
import functools

import jax
import jax.numpy as jnp
from jax import lax
from jax.experimental import pallas as pl
from jax.experimental.pallas import tpu as pltpu
from jax.sharding import PartitionSpec as P

B = 32
TILES = B * B // 128
stretch_step = 0.25

AFTER_Y, AFTER_Z, U1_Y, U1_Z, U2_Z = 0, 3, 6, 7, 8
FACES = 9
EXTRA = FACES
SPILLS = 6
KEPT = (0, 1, 2, 5, 6, 7)
PACKED = len(KEPT)
ROW_U1_Y, ROW_U1_Z, ROW_U2_Z, ROW_CORNER, ROW_BESIDE = 0, 2, 4, 6, 7
SENT = SPILLS + 1 + PACKED
CROSSED = (2, 6)


def iotas():
    return (
        lax.broadcasted_iota(jnp.int32, (8, 128), 0),
        lax.broadcasted_iota(jnp.int32, (8, 128), 1),
    )


def weights(u):
    a = jnp.abs(u)
    rest = 1.0 - a
    centre = 1.0 + a * a * (1.5 * a - 2.5)
    toward = a * (0.5 + a * (2.0 - 1.5 * a))
    away = -0.5 * a * rest * rest
    far = -0.5 * a * a * rest
    up = u >= 0.0
    return {
        0: centre,
        1: jnp.where(up, toward, away),
        -1: jnp.where(up, away, toward),
        2: jnp.where(up, far, 0.0),
        -2: jnp.where(up, 0.0, far),
    }


def lane(tile):
    return pl.ds(128 * tile, 128)


def gathered(tile, index):
    return jnp.take_along_axis(tile, index, axis=1)


def row_of(tile, row):
    return jnp.broadcast_to(tile[row : row + 1], (8, 128))


def pair_rows(tile, row):
    rows, _ = iotas()
    return jnp.where(rows & 1 == 0, row_of(tile, row), row_of(tile, row + 1))


def y_face(tiles):
    _, lanes = iotas()
    return jnp.where(lanes < 64, tiles[0], tiles[TILES - 1])


def z_of(n):
    return jnp.where(n < 2, n, B - 4 + n)


def z_face(tiles):
    _, lanes = iotas()
    index = 32 * ((lanes >> 2) & 3) + z_of(lanes & 3)
    face = None
    for t, tile in enumerate(tiles):
        if tile is not None:
            picked = gathered(tile, index)
            face = picked if face is None else jnp.where((lanes >> 4) == t, picked, face)
    return face


def y_edges(tile):
    _, lanes = iotas()
    y = lanes >> 2
    n = jnp.where(y < 2, y, jnp.where(y >= B - 2, y - (B - 4), 0))
    return gathered(tile, 32 * n + z_of(lanes & 3))


def pack(tiles):
    rows, _ = iotas()
    packed = []
    for j, t in enumerate(KEPT):
        last = jnp.where(rows == 6, pltpu.roll(tiles[3], 6 - j, 0), pltpu.roll(tiles[4], 7 - j, 0))
        packed.append(jnp.where(rows < 6, tiles[t], last))
    return packed


def unpack(packed):
    rows, _ = iotas()
    tiles = dict(zip(KEPT, packed))
    for t, row in ((3, 6), (4, 7)):
        tiles[t] = packed[0]
        for j, tile in enumerate(packed):
            tiles[t] = jnp.where(rows == j, pltpu.roll(tile, (j - row) % 8, 0), tiles[t])
    return [tiles[t] for t in range(TILES)]


def placed(tile, c, row):
    rows, _ = iotas()
    moved = pltpu.roll(tile, (row - 2 * c + 8) % 8, 0)
    return jnp.where((rows >= row) & (rows < row + 2), moved, 0.0)


def y_spill(fields, u):
    _, lanes = iotas()
    weight = weights(u)
    low = lanes < 64
    one = jnp.where(low, weight[-1], weight[1])
    two = jnp.where(low, weight[-2], weight[2])
    spilt = []
    for q in fields:
        q1, q2 = q * one, q * two
        edge = jnp.where(lanes < 32, pltpu.roll(q1, 32, 1), pltpu.roll(q1, 96, 1))
        edge = jnp.where((lanes < 32) | (lanes >= 96), edge, 0.0)
        spilt.append(pltpu.roll(q2, 64, 1) + edge)
    return spilt


def z_spill(fields, u):
    _, lanes = iotas()
    n = lanes & 3
    weight = weights(u)
    one = jnp.where(n < 2, weight[-1], weight[1])
    two = jnp.where(n < 2, weight[-2], weight[2])
    spilt = []
    for q in fields:
        q1, q2 = q * one, q * two
        edge = jnp.where(n == 0, pltpu.roll(q1, 125, 1), pltpu.roll(q1, 3, 1))
        edge = jnp.where((n == 0) | (n == 3), edge, 0.0)
        spilt.append(jnp.where(n < 2, pltpu.roll(q2, 126, 1), pltpu.roll(q2, 2, 1)) + edge)
    return spilt


def y_pass_of_z_face(q, weight, beside=None, beside_weight=None):
    _, lanes = iotas()
    y = lanes >> 2
    total = q * weight[0]
    for k in (-2, -1, 1, 2):
        outside = y >= B - k if k > 0 else y < -k
        other = 0.0 if beside is None else beside * beside_weight[k]
        total = total + pltpu.roll(jnp.where(outside, other, q * weight[k]), (4 * k) % 128, 1)
    return total


def stretched(w_ref, g_ref, t):
    w = [w_ref[c, 0, :, lane(t)] for c in range(3)]
    return [
        w[c]
        + stretch_step
        * (
            g_ref[3 * c, 0, :, lane(t)] * w[0]
            + g_ref[3 * c + 1, 0, :, lane(t)] * w[1]
            + g_ref[3 * c + 2, 0, :, lane(t)] * w[2]
        )
        for c in range(3)
    ]


def spill_kernel(slab, *refs):
    here, (w_ref, u_ref, g_ref, up_ref, down_ref, meta_ref) = refs[:4], refs[4:10]
    nb_ref, sems = refs[10:]
    copies = [
        pltpu.make_async_copy(source, target, sems.at[n])
        for n, (source, target) in enumerate(zip(here, (nb_ref, w_ref, u_ref, g_ref)))
    ]
    for copy in copies:
        copy.start()
    for copy in copies:
        copy.wait()
    rows, lanes = iotas()
    ups, downs = [], []
    for t in range(TILES):
        q = stretched(w_ref, g_ref, t)
        u = u_ref[0, 0, :, lane(t)]
        top, bottom = q[2], q[2]
        for c in (2, 1, 0):
            mine = rows < 2 * c + 2
            shift = (2 * c + 2 - slab) % 8
            top = jnp.where(mine, pltpu.roll(q[c], shift, 0) if shift else q[c], top)
            bottom = jnp.where(mine, pltpu.roll(q[c], 2 * c, 0) if c else q[c], bottom)
        weight = weights(pair_rows(u, slab - 2))
        edge = jnp.where(rows & 1 == 0, pltpu.roll(top * weight[1], 7, 0), 0.0)
        ups.append(top * weight[2] + edge)
        weight = weights(pair_rows(u, 0))
        edge = jnp.where(rows & 1 == 1, pltpu.roll(bottom * weight[-1], 1, 0), 0.0)
        downs.append(bottom * weight[-2] + edge)
    for j, (up, down) in enumerate(zip(pack(ups), pack(downs))):
        up_ref[j], down_ref[j] = up, down
    meta = jnp.zeros((8, 128), jnp.float32)
    for j in range(6):
        meta = jnp.where(lanes == j, nb_ref[0, j].astype(jnp.float32), meta)
    meta_ref[...] = meta


def inside_kernel(slab, slabs, w_ref, u_ref, g_ref, meta_ref, after_ref, face_ref):
    rows, lanes = iotas()
    after = [[], [], []]
    for t in range(TILES):
        weight = weights(u_ref[0, 0, :, lane(t)])
        for c, q in enumerate(stretched(w_ref, g_ref, t)):
            inside = q * weight[0]
            for k in (1, 2):
                spilt = rows < k if slab == 8 else rows >= slab
                inside = inside + jnp.where(spilt, 0.0, pltpu.roll(q * weight[k], k, 0))
                spilt = rows >= 8 - k
                inside = inside + jnp.where(spilt, 0.0, pltpu.roll(q * weight[-k], 8 - k, 0))
            after[c].append(inside)
            after_ref[c, :, lane(t)] = inside
    u1 = [u_ref[1, 0, :, lane(t)] for t in range(TILES)]
    u2 = [u_ref[2, 0, :, lane(t)] for t in range(TILES)]
    faces = [y_face(after[c]) for c in range(3)] + [z_face(after[c]) for c in range(3)]
    faces += [y_face(u1), z_face(u1), z_face(u2)]
    faces.append(extra_of(slab, slabs, faces, meta_ref[...]))
    weight = weights(faces[U1_Z])
    in_z = [y_pass_of_z_face(q, weight) for q in faces[AFTER_Z : AFTER_Z + 3]]
    faces[:SPILLS] = y_spill(faces[:AFTER_Z], faces[U1_Y]) + z_spill(in_z, faces[U2_Z])
    for n, face in enumerate(faces):
        face_ref[n] = face


def extra_of(slab, slabs, faces, meta):
    rows, lanes = iotas()
    far_row = jnp.where(lax.axis_index("sub") == slabs - 1, slab - 2, 0)
    corner = gathered(faces[U2_Z], 4 * z_of((lanes >> 2) & 3) + (lanes & 3))
    corner = jnp.sum(jnp.where(rows == lanes >> 4, corner, 0.0), axis=0, keepdims=True)
    extra = jnp.where(rows < ROW_BESIDE, jnp.broadcast_to(corner, (8, 128)), meta)
    for tile, row in ((U2_Z, ROW_U2_Z), (U1_Z, ROW_U1_Z), (U1_Y, ROW_U1_Y)):
        moved = pltpu.roll(faces[tile], (row - far_row + 8) % 8, 0)
        extra = jnp.where(rows < row + 2, moved, extra)
    return extra


def spills_of(slab, face_ref, up, down):
    spilt = [face_ref[n] for n in range(SPILLS)]
    for packed, row in ((up, 0), (down, slab - 2)):
        tiles = unpack(packed)
        u1_y, u1_z, u2_z = (pair_rows(face_ref[n], row) for n in (U1_Y, U1_Z, U2_Z))
        (by_y,) = y_spill([y_face(tiles)], u1_y)
        (by_z,) = z_spill([y_pass_of_z_face(z_face(tiles), weights(u1_z))], u2_z)
        for c in range(3):
            spilt[c] = spilt[c] + placed(by_y, c, row)
            spilt[3 + c] = spilt[3 + c] + placed(by_z, c, row)
    return spilt


def middle_kernel(slab, slabs, face_ref, own_face_ref, up_ref, down_ref, sent_ref, own_sent_ref):
    first, last = lax.axis_index("sub") == 0, lax.axis_index("sub") == slabs - 1
    up, down, far = [], [], []
    for j in range(PACKED):
        up.append(jnp.where(first, 0.0, up_ref[j]))
        down.append(jnp.where(last, 0.0, down_ref[j]))
        far.append(jnp.where(first, up_ref[j], jnp.where(last, down_ref[j], 0.0)))
    sent = spills_of(slab, face_ref, up, down) + [own_face_ref[EXTRA]] + far
    for n, tile in enumerate(sent):
        sent_ref[n] = tile
    for n, tile in enumerate(sent + up + down):
        own_sent_ref[n] = tile


def y_pass(fields, weight):
    _, lanes = iotas()
    results = []
    for tiles in fields:
        moved = {
            (t, k): pltpu.roll(tiles[t] * weight[t][k], (32 * k) % 128, 1)
            for t in range(TILES)
            for k in (-2, -1, 1, 2)
        }
        result = []
        for t in range(TILES):
            total = tiles[t] * weight[t][0]
            for k in (1, 2):
                other = moved[t - 1, k] if t > 0 else 0.0
                total = total + jnp.where(lanes < 32 * k, other, moved[t, k])
                other = moved[t + 1, -k] if t < TILES - 1 else 0.0
                total = total + jnp.where(lanes >= 128 - 32 * k, other, moved[t, -k])
            result.append(total)
        results.append(result)
    return results


def z_pass(q, weight):
    _, lanes = iotas()
    z = lanes & 31
    total = q * weight[0]
    for k in (1, 2):
        total = total + jnp.where(z >= k, pltpu.roll(q * weight[k], k, 1), 0.0)
        total = total + jnp.where(z < B - k, pltpu.roll(q * weight[-k], 128 - k, 1), 0.0)
    return total


def own_kernel(slab, after_ref, u_ref, near_ref, own_ref):
    up = unpack([near_ref[SENT + j] for j in range(PACKED)])
    down = unpack([near_ref[SENT + PACKED + j] for j in range(PACKED)])
    after = [
        [
            after_ref[c, :, lane(t)] + placed(up[t], c, 0) + placed(down[t], c, slab - 2)
            for t in range(TILES)
        ]
        for c in range(3)
    ]
    after = y_pass(after, [weights(u_ref[1, 0, :, lane(t)]) for t in range(TILES)])
    for t in range(TILES):
        weight = weights(u_ref[2, 0, :, lane(t)])
        for c in range(3):
            own_ref[c, :, lane(t)] = z_pass(after[c][t], weight)


def last_kernel(slab, slabs, paired, own_ref, u_ref, *refs):
    block_refs, out_ref = refs[:-1], refs[-1]
    rows, lanes = iotas()
    here = lax.axis_index("blk")
    place_in = lax.axis_index("sub")
    below_x = place_in == 0
    above_x = place_in == slabs - 1
    at_end = below_x | above_x
    far_row = jnp.where(above_x, slab - 2, 0)
    x_face = jnp.where(above_x, 1, 0)
    second = here % 2 == 1
    base = here - here % 2 if paired else 0

    def over_blocks(step, carry):
        if not paired:
            (ref,) = block_refs
            return lax.fori_loop(
                0,
                ref.shape[0],
                lambda slot, c: step(
                    slot,
                    lambda n: ref[slot, n],
                    lambda j: ref[slot, SPILLS + 1 + j],
                    lambda: ref[slot, SPILLS],
                    c,
                ),
                carry,
            )
        for slot in range(2 * chips):
            n, p = slot // 2, slot % 2
            carry = step(
                slot,
                lambda i, n=n, p=p: prepared(n, p, i),
                lambda j, n=n, p=p: prepared(n, p, SPILLS + 1 + j),
                lambda n=n, p=p: prepared(n, p, SPILLS),
                carry,
            )
        return carry

    chips = len(block_refs) // 2

    def prepared(n, p, tile):
        held, other = block_refs[n][tile], block_refs[chips + n][tile]
        held_by_second = (p == 1) == (2 * n not in CROSSED)
        return jnp.where(second, held, other) if held_by_second else jnp.where(second, other, held)

    own_extra = block_refs[0][SPILLS] if paired else block_refs[0][here, SPILLS]

    def beside(extra, face):
        index = jnp.full((8, 128), face, jnp.int32)
        return gathered(row_of(extra, ROW_BESIDE), index).astype(jnp.int32) ^ base

    ym, yp, zm, zp = (beside(own_extra, face) for face in (2, 3, 4, 5))
    outer = jnp.where(at_end, beside(own_extra, x_face), here ^ base)

    def find_corners(slot, spills, far, extra, found):
        tile = extra()
        below, above = (beside(tile, face) for face in (2, 3))
        at_m, at_p = zm == slot, zp == slot
        mm, mp, pm, pp = found
        return (
            jnp.where(at_m, below, mm),
            jnp.where(at_m, above, mp),
            jnp.where(at_p, below, pm),
            jnp.where(at_p, above, pp),
        )

    zmm, zmp, zpm, zpp = over_blocks(find_corners, (zm, zm, zp, zp))
    near_slots = (ym, yp, zm, zp, zmm, zmp, zpm, zpp)

    def find_far(slot, spills, far, extra, found):
        there = beside(extra(), x_face)
        return tuple(
            jnp.where(at_end & (start == slot), there, f) for start, f in zip(near_slots, found)
        )

    far_ym, far_yp, far_zm, far_zp, far_zmm, far_zmp, far_zpm, far_zpp = over_blocks(
        find_far, near_slots
    )

    y_low = lanes < 64
    n_low = lanes & 3 < 2
    z_cell = lanes & 31
    z_low = z_cell < 16
    corner_low, corner_high = jnp.where(z_low, zpm, zmm), jnp.where(z_low, zpp, zmp)
    wanted_spills = (
        [(jnp.where(y_low, ym, yp), n) for n in (0, 1, 2)]
        + [(jnp.where(n_low, zm, zp), n) for n in (3, 4, 5)]
        + [(jnp.where(y_low, corner_low, corner_high), n) for n in (0, 1, 2)]
    )
    wanted_extra = [
        jnp.where(y_low, yp, ym),
        jnp.where(n_low, zp, zm),
        jnp.where(y_low, corner_high, corner_low),
    ]
    far_z = jnp.where(z_low, far_zp, far_zm)
    wanted_far = (
        [(far_yp, 0), (far_ym, PACKED - 1)]
        + [(jnp.where(z_low, far_zpp, far_zmp), 0)]
        + [(jnp.where(z_low, far_zpm, far_zmm), PACKED - 1)]
        + [(far_z, j) for j in range(PACKED)]
        + [(outer, j) for j in range(PACKED)]
    )

    def pick(slot, spills, far, extra, picked):
        tile = extra()
        found = [(which, spills(n)) for which, n in wanted_spills]
        found += [(which, tile) for which in wanted_extra]
        found += [(which, far(j)) for which, j in wanted_far]
        return tuple(jnp.where(which == slot, t, p) for (which, t), p in zip(found, picked))

    count = len(wanted_spills) + len(wanted_extra) + len(wanted_far)
    picked = list(over_blocks(pick, (jnp.zeros((8, 128), jnp.float32),) * count))
    into_y, into_z, into_corner = picked[0:3], picked[3:6], picked[6:9]
    extra_y, extra_z, extra_c = picked[9:12]
    far_y = jnp.where(y_low, picked[12], picked[13])
    far_c = z_face([picked[14]] + [None] * (TILES - 2) + [picked[15]])
    far_z = z_face(unpack(picked[16 : 16 + PACKED]))
    far_own = unpack(picked[16 + PACKED :])

    (by_far,) = y_spill([far_y], pair_rows(extra_y, ROW_U1_Y))
    into_y = [into_y[c] + placed(by_far, c, far_row) for c in range(3)]

    (by_far,) = z_spill(
        [
            y_pass_of_z_face(
                far_z,
                weights(pair_rows(extra_z, ROW_U1_Z)),
                far_c,
                weights(y_edges(pair_rows(extra_c, ROW_U1_Y))),
            )
        ],
        pair_rows(extra_z, ROW_U2_Z),
    )
    y = lanes >> 2
    at_edge = (y < 2) | (y >= B - 2)
    n = jnp.where(y < 2, y, jnp.where(y >= B - 2, y - (B - 4), 0))
    u2 = gathered(row_of(extra_z, ROW_CORNER), 16 * rows + 4 * n + (lanes & 3))
    by_corner = z_spill([jnp.where(at_edge, y_edges(q), 0.0) for q in into_corner], u2)
    into_z = [into_z[c] + by_corner[c] + placed(by_far, c, far_row) for c in range(3)]

    def far_rows(c, t):
        u = pltpu.roll(u_ref[c, 0, :, lane(t)], (8 - far_row) % 8, 0)
        return weights(pair_rows(u, 0))

    packed = y_pass([far_own], [far_rows(1, t) for t in range(TILES)])[0]
    packed = [z_pass(packed[t], far_rows(2, t)) for t in range(TILES)]
    u2 = y_face([u_ref[2, 0, :, lane(t)] for t in range(TILES)])
    weight = weights(u2)
    into_y = [z_pass(q, weight) for q in into_y]
    at_face = (z_cell < 2) | (z_cell >= B - 2)
    place = jnp.where(z_cell < 2, z_cell, jnp.where(z_cell >= B - 2, z_cell - (B - 4), 0))
    for t in range(TILES):
        index = 16 * t + 4 * (lanes >> 5) + place
        for c in range(3):
            total = own_ref[c, :, lane(t)] + placed(packed[t], c, far_row)
            if t == 0:
                total = total + jnp.where(y_low, into_y[c], 0.0)
            if t == TILES - 1:
                total = total + jnp.where(y_low, 0.0, into_y[c])
            out_ref[c, 0, :, lane(t)] = total + jnp.where(at_face, gathered(into_z[c], index), 0.0)


def shards(slabs, vorticity, velocity, gradient, neighbour):
    slab = vorticity.shape[2]
    if slab < 8:
        room = ((0, 0), (0, 0), (0, 8 - slab), (0, 0))
        vorticity, velocity, gradient = (
            jnp.pad(a, room) for a in (vorticity, velocity, gradient)
        )
    blocks = lax.axis_size("blk")
    paired = blocks in (2, 4, 8)
    vmem = pl.BlockSpec(memory_space=pltpu.VMEM)
    hbm = pl.BlockSpec(memory_space=pltpu.HBM)
    small = pltpu.CompilerParams(vmem_limit_bytes=16 << 20)

    def shape(*dims):
        return jax.ShapeDtypeStruct(dims, jnp.float32)

    def tiles(count):
        return shape(count, 8, 128)

    def call(kernel, out_shape, *args, params=small):
        return pl.pallas_call(
            kernel,
            out_shape=out_shape,
            in_specs=[vmem] * len(args),
            out_specs=(vmem,) * len(out_shape) if isinstance(out_shape, tuple) else vmem,
            compiler_params=params,
        )(*args)

    inputs = (neighbour, vorticity, velocity, gradient)
    vorticity, velocity, gradient, up, down, meta = pl.pallas_call(
        functools.partial(spill_kernel, slab),
        out_shape=(
            shape(*vorticity.shape),
            shape(*velocity.shape),
            shape(*gradient.shape),
            tiles(PACKED),
            tiles(PACKED),
            shape(8, 128),
        ),
        in_specs=[hbm] * 4,
        out_specs=(vmem,) * 6,
        scratch_shapes=[
            pltpu.SMEM(neighbour.shape, jnp.int32),
            pltpu.SemaphoreType.DMA((4,)),
        ],
        compiler_params=small,
    )(*(pltpu.with_memory_space_constraint(a, pltpu.HBM) for a in inputs))
    after, faces = call(
        functools.partial(inside_kernel, slab, slabs),
        (shape(3, 8, B * B), tiles(FACES + 1)),
        vorticity,
        velocity,
        gradient,
        meta,
    )

    def moved(array, d, step=0):
        pairs = []
        for b in range(blocks):
            for s in range(slabs):
                c = b ^ d
                pairs.append((b * slabs + s, c * slabs + (s + step) % slabs))
        return lax.ppermute(array, ("blk", "sub"), pairs)

    cross = 0
    up = moved(up, cross, 1)
    down = moved(down, cross, -1)
    their_faces = faces
    sent, near = call(
        functools.partial(middle_kernel, slab, slabs),
        (tiles(SENT), tiles(SENT + 2 * PACKED)),
        their_faces,
        faces,
        up,
        down,
    )
    if paired:
        held, theirs = [sent], [moved(sent, 1)]
        for d in range(2, blocks, 2):
            held.append(moved(sent, d ^ (d in CROSSED)))
            theirs.append(moved(sent, d ^ (d not in CROSSED)) if d == 2 else moved(held[-1], 1))
        arrays = held + theirs
    else:
        arrays = [lax.all_gather(sent, "blk")]
    own = call(
        functools.partial(own_kernel, slab), shape(3, 8, B * B), after, velocity, near
    )
    room = (16 << 20) + (0 if paired else arrays[0].size * 4)
    out = call(
        functools.partial(last_kernel, slab, slabs, paired),
        shape(3, 1, 8, B * B),
        own,
        velocity,
        *arrays,
        params=pltpu.CompilerParams(vmem_limit_bytes=room),
    )
    return out[:, :, :slab]


def solution(mesh):
    return jax.shard_map(
        functools.partial(shards, mesh.shape["sub"]),
        mesh=mesh,
        in_specs=(
            P(None, "blk", "sub", None),
            P(None, "blk", "sub", None),
            P(None, "blk", "sub", None),
            P("blk", None),
        ),
        out_specs=P(None, "blk", "sub", None),
        check_vma=False,
    )
```

```python
import functools

import jax
import jax.numpy as jnp
from jax import lax
from jax.experimental import pallas as pl
from jax.experimental.pallas import tpu as pltpu
from jax.sharding import PartitionSpec as P

B = 32
TILES = B * B // 128
stretch_step = 0.25

AFTER_Y, AFTER_Z, U1_Y, U1_Z, U2_Z = 0, 3, 6, 7, 8
FACES = 9
EXTRA = FACES
SPILLS = 6
KEPT = (0, 1, 2, 5, 6, 7)
PACKED = len(KEPT)
ROW_U1_Y, ROW_U1_Z, ROW_U2_Z, ROW_CORNER, ROW_BESIDE = 0, 2, 4, 6, 7
SENT = SPILLS + 1 + PACKED
CROSSED = (2, 6)


def iotas():
    return (
        lax.broadcasted_iota(jnp.int32, (8, 128), 0),
        lax.broadcasted_iota(jnp.int32, (8, 128), 1),
    )


def weights(u):
    a = jnp.abs(u)
    rest = 1.0 - a
    centre = 1.0 + a * a * (1.5 * a - 2.5)
    toward = a * (0.5 + a * (2.0 - 1.5 * a))
    away = -0.5 * a * rest * rest
    far = -0.5 * a * a * rest
    up = u >= 0.0
    return {
        0: centre,
        1: jnp.where(up, toward, away),
        -1: jnp.where(up, away, toward),
        2: jnp.where(up, far, 0.0),
        -2: jnp.where(up, 0.0, far),
    }


def lane(tile):
    return pl.ds(128 * tile, 128)


def gathered(tile, index):
    return jnp.take_along_axis(tile, index, axis=1)


def row_of(tile, row):
    return jnp.broadcast_to(tile[row : row + 1], (8, 128))


def pair_rows(tile, row):
    rows, _ = iotas()
    return jnp.where(rows & 1 == 0, row_of(tile, row), row_of(tile, row + 1))


def y_face(tiles):
    _, lanes = iotas()
    return jnp.where(lanes < 64, tiles[0], tiles[TILES - 1])


def z_of(n):
    return jnp.where(n < 2, n, B - 4 + n)


def z_face(tiles):
    _, lanes = iotas()
    index = 32 * ((lanes >> 2) & 3) + z_of(lanes & 3)
    face = None
    for t, tile in enumerate(tiles):
        if tile is not None:
            picked = gathered(tile, index)
            face = picked if face is None else jnp.where((lanes >> 4) == t, picked, face)
    return face


def y_edges(tile):
    _, lanes = iotas()
    y = lanes >> 2
    n = jnp.where(y < 2, y, jnp.where(y >= B - 2, y - (B - 4), 0))
    return gathered(tile, 32 * n + z_of(lanes & 3))


def pack(tiles):
    rows, _ = iotas()
    packed = []
    for j, t in enumerate(KEPT):
        last = jnp.where(rows == 6, pltpu.roll(tiles[3], 6 - j, 0), pltpu.roll(tiles[4], 7 - j, 0))
        packed.append(jnp.where(rows < 6, tiles[t], last))
    return packed


def unpack(packed):
    rows, _ = iotas()
    tiles = dict(zip(KEPT, packed))
    for t, row in ((3, 6), (4, 7)):
        tiles[t] = packed[0]
        for j, tile in enumerate(packed):
            tiles[t] = jnp.where(rows == j, pltpu.roll(tile, (j - row) % 8, 0), tiles[t])
    return [tiles[t] for t in range(TILES)]


def placed(tile, c, row):
    rows, _ = iotas()
    moved = pltpu.roll(tile, (row - 2 * c + 8) % 8, 0)
    return jnp.where((rows >= row) & (rows < row + 2), moved, 0.0)


def y_spill(fields, u):
    _, lanes = iotas()
    weight = weights(u)
    low = lanes < 64
    one = jnp.where(low, weight[-1], weight[1])
    two = jnp.where(low, weight[-2], weight[2])
    spilt = []
    for q in fields:
        q1, q2 = q * one, q * two
        edge = jnp.where(lanes < 32, pltpu.roll(q1, 32, 1), pltpu.roll(q1, 96, 1))
        edge = jnp.where((lanes < 32) | (lanes >= 96), edge, 0.0)
        spilt.append(pltpu.roll(q2, 64, 1) + edge)
    return spilt


def z_spill(fields, u):
    _, lanes = iotas()
    n = lanes & 3
    weight = weights(u)
    one = jnp.where(n < 2, weight[-1], weight[1])
    two = jnp.where(n < 2, weight[-2], weight[2])
    spilt = []
    for q in fields:
        q1, q2 = q * one, q * two
        edge = jnp.where(n == 0, pltpu.roll(q1, 125, 1), pltpu.roll(q1, 3, 1))
        edge = jnp.where((n == 0) | (n == 3), edge, 0.0)
        spilt.append(jnp.where(n < 2, pltpu.roll(q2, 126, 1), pltpu.roll(q2, 2, 1)) + edge)
    return spilt


def y_pass_of_z_face(q, weight, beside=None, beside_weight=None):
    _, lanes = iotas()
    y = lanes >> 2
    total = q * weight[0]
    for k in (-2, -1, 1, 2):
        outside = y >= B - k if k > 0 else y < -k
        other = 0.0 if beside is None else beside * beside_weight[k]
        total = total + pltpu.roll(jnp.where(outside, other, q * weight[k]), (4 * k) % 128, 1)
    return total


def stretched(w_ref, g_ref, t):
    w = [w_ref[c, 0, :, lane(t)] for c in range(3)]
    return [
        w[c]
        + stretch_step
        * (
            g_ref[3 * c, 0, :, lane(t)] * w[0]
            + g_ref[3 * c + 1, 0, :, lane(t)] * w[1]
            + g_ref[3 * c + 2, 0, :, lane(t)] * w[2]
        )
        for c in range(3)
    ]


def spill_kernel(slab, *refs):
    here, (w_ref, u_ref, g_ref, up_ref, down_ref, meta_ref) = refs[:4], refs[4:10]
    nb_ref, sems = refs[10:]
    copies = [
        pltpu.make_async_copy(source, target, sems.at[n])
        for n, (source, target) in enumerate(zip(here, (nb_ref, w_ref, u_ref, g_ref)))
    ]
    for copy in copies[::-1]:
        copy.start()
    for copy in copies:
        copy.wait()
    rows, lanes = iotas()
    ups, downs = [], []
    for t in range(TILES):
        q = stretched(w_ref, g_ref, t)
        u = u_ref[0, 0, :, lane(t)]
        top, bottom = q[2], q[2]
        for c in (2, 1, 0):
            mine = rows < 2 * c + 2
            shift = (2 * c + 2 - slab) % 8
            top = jnp.where(mine, pltpu.roll(q[c], shift, 0) if shift else q[c], top)
            bottom = jnp.where(mine, pltpu.roll(q[c], 2 * c, 0) if c else q[c], bottom)
        weight = weights(pair_rows(u, slab - 2))
        edge = jnp.where(rows & 1 == 0, pltpu.roll(top * weight[1], 7, 0), 0.0)
        ups.append(top * weight[2] + edge)
        weight = weights(pair_rows(u, 0))
        edge = jnp.where(rows & 1 == 1, pltpu.roll(bottom * weight[-1], 1, 0), 0.0)
        downs.append(bottom * weight[-2] + edge)
    for j, (up, down) in enumerate(zip(pack(ups), pack(downs))):
        up_ref[j], down_ref[j] = up, down
    meta = jnp.zeros((8, 128), jnp.float32)
    for j in range(6):
        meta = jnp.where(lanes == j, nb_ref[0, j].astype(jnp.float32), meta)
    meta_ref[...] = meta


def inside_kernel(slab, slabs, w_ref, u_ref, g_ref, meta_ref, after_ref, face_ref):
    rows, lanes = iotas()
    after = [[], [], []]
    for t in range(TILES):
        weight = weights(u_ref[0, 0, :, lane(t)])
        for c, q in enumerate(stretched(w_ref, g_ref, t)):
            inside = q * weight[0]
            for k in (1, 2):
                spilt = rows < k if slab == 8 else rows >= slab
                inside = inside + jnp.where(spilt, 0.0, pltpu.roll(q * weight[k], k, 0))
                spilt = rows >= 8 - k
                inside = inside + jnp.where(spilt, 0.0, pltpu.roll(q * weight[-k], 8 - k, 0))
            after[c].append(inside)
            after_ref[c, :, lane(t)] = inside
    u1 = [u_ref[1, 0, :, lane(t)] for t in range(TILES)]
    u2 = [u_ref[2, 0, :, lane(t)] for t in range(TILES)]
    faces = [y_face(after[c]) for c in range(3)] + [z_face(after[c]) for c in range(3)]
    faces += [y_face(u1), z_face(u1), z_face(u2)]
    faces.append(extra_of(slab, slabs, faces, meta_ref[...]))
    weight = weights(faces[U1_Z])
    in_z = [y_pass_of_z_face(q, weight) for q in faces[AFTER_Z : AFTER_Z + 3]]
    faces[:SPILLS] = y_spill(faces[:AFTER_Z], faces[U1_Y]) + z_spill(in_z, faces[U2_Z])
    for n, face in enumerate(faces):
        face_ref[n] = face


def extra_of(slab, slabs, faces, meta):
    rows, lanes = iotas()
    far_row = jnp.where(lax.axis_index("sub") == slabs - 1, slab - 2, 0)
    corner = gathered(faces[U2_Z], 4 * z_of((lanes >> 2) & 3) + (lanes & 3))
    corner = jnp.sum(jnp.where(rows == lanes >> 4, corner, 0.0), axis=0, keepdims=True)
    extra = jnp.where(rows < ROW_BESIDE, jnp.broadcast_to(corner, (8, 128)), meta)
    for tile, row in ((U2_Z, ROW_U2_Z), (U1_Z, ROW_U1_Z), (U1_Y, ROW_U1_Y)):
        moved = pltpu.roll(faces[tile], (row - far_row + 8) % 8, 0)
        extra = jnp.where(rows < row + 2, moved, extra)
    return extra


def spills_of(slab, face_ref, up, down):
    spilt = [face_ref[n] for n in range(SPILLS)]
    for packed, row in ((up, 0), (down, slab - 2)):
        tiles = unpack(packed)
        u1_y, u1_z, u2_z = (pair_rows(face_ref[n], row) for n in (U1_Y, U1_Z, U2_Z))
        (by_y,) = y_spill([y_face(tiles)], u1_y)
        (by_z,) = z_spill([y_pass_of_z_face(z_face(tiles), weights(u1_z))], u2_z)
        for c in range(3):
            spilt[c] = spilt[c] + placed(by_y, c, row)
            spilt[3 + c] = spilt[3 + c] + placed(by_z, c, row)
    return spilt


def middle_kernel(slab, slabs, face_ref, own_face_ref, up_ref, down_ref, sent_ref, own_sent_ref):
    first, last = lax.axis_index("sub") == 0, lax.axis_index("sub") == slabs - 1
    up, down, far = [], [], []
    for j in range(PACKED):
        up.append(jnp.where(first, 0.0, up_ref[j]))
        down.append(jnp.where(last, 0.0, down_ref[j]))
        far.append(jnp.where(first, up_ref[j], jnp.where(last, down_ref[j], 0.0)))
    sent = spills_of(slab, face_ref, up, down) + [own_face_ref[EXTRA]] + far
    for n, tile in enumerate(sent):
        sent_ref[n] = tile
    for n, tile in enumerate(sent + up + down):
        own_sent_ref[n] = tile


def y_pass(fields, weight):
    _, lanes = iotas()
    results = []
    for tiles in fields:
        moved = {
            (t, k): pltpu.roll(tiles[t] * weight[t][k], (32 * k) % 128, 1)
            for t in range(TILES)
            for k in (-2, -1, 1, 2)
        }
        result = []
        for t in range(TILES):
            total = tiles[t] * weight[t][0]
            for k in (1, 2):
                other = moved[t - 1, k] if t > 0 else 0.0
                total = total + jnp.where(lanes < 32 * k, other, moved[t, k])
                other = moved[t + 1, -k] if t < TILES - 1 else 0.0
                total = total + jnp.where(lanes >= 128 - 32 * k, other, moved[t, -k])
            result.append(total)
        results.append(result)
    return results


def z_pass(q, weight):
    _, lanes = iotas()
    z = lanes & 31
    total = q * weight[0]
    for k in (1, 2):
        total = total + jnp.where(z >= k, pltpu.roll(q * weight[k], k, 1), 0.0)
        total = total + jnp.where(z < B - k, pltpu.roll(q * weight[-k], 128 - k, 1), 0.0)
    return total


def own_kernel(slab, after_ref, u_ref, near_ref, own_ref):
    up = unpack([near_ref[SENT + j] for j in range(PACKED)])
    down = unpack([near_ref[SENT + PACKED + j] for j in range(PACKED)])
    after = [
        [
            after_ref[c, :, lane(t)] + placed(up[t], c, 0) + placed(down[t], c, slab - 2)
            for t in range(TILES)
        ]
        for c in range(3)
    ]
    after = y_pass(after, [weights(u_ref[1, 0, :, lane(t)]) for t in range(TILES)])
    for t in range(TILES):
        weight = weights(u_ref[2, 0, :, lane(t)])
        for c in range(3):
            own_ref[c, :, lane(t)] = z_pass(after[c][t], weight)


def last_kernel(slab, slabs, paired, own_ref, u_ref, *refs):
    block_refs, out_ref = refs[:-1], refs[-1]
    rows, lanes = iotas()
    here = lax.axis_index("blk")
    place_in = lax.axis_index("sub")
    below_x = place_in == 0
    above_x = place_in == slabs - 1
    at_end = below_x | above_x
    far_row = jnp.where(above_x, slab - 2, 0)
    x_face = jnp.where(above_x, 1, 0)
    second = here % 2 == 1
    base = here - here % 2 if paired else 0

    def over_blocks(step, carry):
        if not paired:
            (ref,) = block_refs
            return lax.fori_loop(
                0,
                ref.shape[0],
                lambda slot, c: step(
                    slot,
                    lambda n: ref[slot, n],
                    lambda j: ref[slot, SPILLS + 1 + j],
                    lambda: ref[slot, SPILLS],
                    c,
                ),
                carry,
            )
        for slot in range(2 * chips):
            n, p = slot // 2, slot % 2
            carry = step(
                slot,
                lambda i, n=n, p=p: prepared(n, p, i),
                lambda j, n=n, p=p: prepared(n, p, SPILLS + 1 + j),
                lambda n=n, p=p: prepared(n, p, SPILLS),
                carry,
            )
        return carry

    chips = len(block_refs) // 2

    def prepared(n, p, tile):
        held, other = block_refs[n][tile], block_refs[chips + n][tile]
        held_by_second = (p == 1) == (2 * n not in CROSSED)
        return jnp.where(second, held, other) if held_by_second else jnp.where(second, other, held)

    own_extra = block_refs[0][SPILLS] if paired else block_refs[0][here, SPILLS]

    def beside(extra, face):
        index = jnp.full((8, 128), face, jnp.int32)
        return gathered(row_of(extra, ROW_BESIDE), index).astype(jnp.int32) ^ base

    ym, yp, zm, zp = (beside(own_extra, face) for face in (2, 3, 4, 5))
    outer = jnp.where(at_end, beside(own_extra, x_face), here ^ base)

    def find_corners(slot, spills, far, extra, found):
        tile = extra()
        below, above = (beside(tile, face) for face in (2, 3))
        at_m, at_p = zm == slot, zp == slot
        mm, mp, pm, pp = found
        return (
            jnp.where(at_m, below, mm),
            jnp.where(at_m, above, mp),
            jnp.where(at_p, below, pm),
            jnp.where(at_p, above, pp),
        )

    zmm, zmp, zpm, zpp = over_blocks(find_corners, (zm, zm, zp, zp))
    near_slots = (ym, yp, zm, zp, zmm, zmp, zpm, zpp)

    def find_far(slot, spills, far, extra, found):
        there = beside(extra(), x_face)
        return tuple(
            jnp.where(at_end & (start == slot), there, f) for start, f in zip(near_slots, found)
        )

    far_ym, far_yp, far_zm, far_zp, far_zmm, far_zmp, far_zpm, far_zpp = over_blocks(
        find_far, near_slots
    )

    y_low = lanes < 64
    n_low = lanes & 3 < 2
    z_cell = lanes & 31
    z_low = z_cell < 16
    corner_low, corner_high = jnp.where(z_low, zpm, zmm), jnp.where(z_low, zpp, zmp)
    wanted_spills = (
        [(jnp.where(y_low, ym, yp), n) for n in (0, 1, 2)]
        + [(jnp.where(n_low, zm, zp), n) for n in (3, 4, 5)]
        + [(jnp.where(y_low, corner_low, corner_high), n) for n in (0, 1, 2)]
    )
    wanted_extra = [
        jnp.where(y_low, yp, ym),
        jnp.where(n_low, zp, zm),
        jnp.where(y_low, corner_high, corner_low),
    ]
    far_z = jnp.where(z_low, far_zp, far_zm)
    wanted_far = (
        [(far_yp, 0), (far_ym, PACKED - 1)]
        + [(jnp.where(z_low, far_zpp, far_zmp), 0)]
        + [(jnp.where(z_low, far_zpm, far_zmm), PACKED - 1)]
        + [(far_z, j) for j in range(PACKED)]
        + [(outer, j) for j in range(PACKED)]
    )

    def pick(slot, spills, far, extra, picked):
        tile = extra()
        found = [(which, spills(n)) for which, n in wanted_spills]
        found += [(which, tile) for which in wanted_extra]
        found += [(which, far(j)) for which, j in wanted_far]
        return tuple(jnp.where(which == slot, t, p) for (which, t), p in zip(found, picked))

    count = len(wanted_spills) + len(wanted_extra) + len(wanted_far)
    picked = list(over_blocks(pick, (jnp.zeros((8, 128), jnp.float32),) * count))
    into_y, into_z, into_corner = picked[0:3], picked[3:6], picked[6:9]
    extra_y, extra_z, extra_c = picked[9:12]
    far_y = jnp.where(y_low, picked[12], picked[13])
    far_c = z_face([picked[14]] + [None] * (TILES - 2) + [picked[15]])
    far_z = z_face(unpack(picked[16 : 16 + PACKED]))
    far_own = unpack(picked[16 + PACKED :])

    (by_far,) = y_spill([far_y], pair_rows(extra_y, ROW_U1_Y))
    into_y = [into_y[c] + placed(by_far, c, far_row) for c in range(3)]

    (by_far,) = z_spill(
        [
            y_pass_of_z_face(
                far_z,
                weights(pair_rows(extra_z, ROW_U1_Z)),
                far_c,
                weights(y_edges(pair_rows(extra_c, ROW_U1_Y))),
            )
        ],
        pair_rows(extra_z, ROW_U2_Z),
    )
    y = lanes >> 2
    at_edge = (y < 2) | (y >= B - 2)
    n = jnp.where(y < 2, y, jnp.where(y >= B - 2, y - (B - 4), 0))
    u2 = gathered(row_of(extra_z, ROW_CORNER), 16 * rows + 4 * n + (lanes & 3))
    by_corner = z_spill([jnp.where(at_edge, y_edges(q), 0.0) for q in into_corner], u2)
    into_z = [into_z[c] + by_corner[c] + placed(by_far, c, far_row) for c in range(3)]

    def far_rows(c, t):
        u = pltpu.roll(u_ref[c, 0, :, lane(t)], (8 - far_row) % 8, 0)
        return weights(pair_rows(u, 0))

    packed = y_pass([far_own], [far_rows(1, t) for t in range(TILES)])[0]
    packed = [z_pass(packed[t], far_rows(2, t)) for t in range(TILES)]
    u2 = y_face([u_ref[2, 0, :, lane(t)] for t in range(TILES)])
    weight = weights(u2)
    into_y = [z_pass(q, weight) for q in into_y]
    at_face = (z_cell < 2) | (z_cell >= B - 2)
    place = jnp.where(z_cell < 2, z_cell, jnp.where(z_cell >= B - 2, z_cell - (B - 4), 0))
    for t in range(TILES):
        index = 16 * t + 4 * (lanes >> 5) + place
        for c in range(3):
            total = own_ref[c, :, lane(t)] + placed(packed[t], c, far_row)
            if t == 0:
                total = total + jnp.where(y_low, into_y[c], 0.0)
            if t == TILES - 1:
                total = total + jnp.where(y_low, 0.0, into_y[c])
            out_ref[c, 0, :, lane(t)] = total + jnp.where(at_face, gathered(into_z[c], index), 0.0)


def shards(slabs, vorticity, velocity, gradient, neighbour):
    slab = vorticity.shape[2]
    if slab < 8:
        room = ((0, 0), (0, 0), (0, 8 - slab), (0, 0))
        vorticity, velocity, gradient = (
            jnp.pad(a, room) for a in (vorticity, velocity, gradient)
        )
    blocks = lax.axis_size("blk")
    paired = blocks in (2, 4, 8)
    vmem = pl.BlockSpec(memory_space=pltpu.VMEM)
    hbm = pl.BlockSpec(memory_space=pltpu.HBM)
    small = pltpu.CompilerParams(vmem_limit_bytes=16 << 20)

    def shape(*dims):
        return jax.ShapeDtypeStruct(dims, jnp.float32)

    def tiles(count):
        return shape(count, 8, 128)

    def call(kernel, out_shape, *args, params=small):
        return pl.pallas_call(
            kernel,
            out_shape=out_shape,
            in_specs=[vmem] * len(args),
            out_specs=(vmem,) * len(out_shape) if isinstance(out_shape, tuple) else vmem,
            compiler_params=params,
        )(*args)

    inputs = (neighbour, vorticity, velocity, gradient)
    vorticity, velocity, gradient, up, down, meta = pl.pallas_call(
        functools.partial(spill_kernel, slab),
        out_shape=(
            shape(*vorticity.shape),
            shape(*velocity.shape),
            shape(*gradient.shape),
            tiles(PACKED),
            tiles(PACKED),
            shape(8, 128),
        ),
        in_specs=[hbm] * 4,
        out_specs=(vmem,) * 6,
        scratch_shapes=[
            pltpu.SMEM(neighbour.shape, jnp.int32),
            pltpu.SemaphoreType.DMA((4,)),
        ],
        compiler_params=small,
    )(*(pltpu.with_memory_space_constraint(a, pltpu.HBM) for a in inputs))
    after, faces = call(
        functools.partial(inside_kernel, slab, slabs),
        (shape(3, 8, B * B), tiles(FACES + 1)),
        vorticity,
        velocity,
        gradient,
        meta,
    )

    def moved(array, d, step=0):
        pairs = []
        for b in range(blocks):
            for s in range(slabs):
                c = b ^ d
                pairs.append((b * slabs + s, c * slabs + (s + step) % slabs))
        return lax.ppermute(array, ("blk", "sub"), pairs)

    cross = 0
    up = moved(up, cross, 1)
    down = moved(down, cross, -1)
    their_faces = faces
    sent, near = call(
        functools.partial(middle_kernel, slab, slabs),
        (tiles(SENT), tiles(SENT + 2 * PACKED)),
        their_faces,
        faces,
        up,
        down,
    )
    if paired:
        held, theirs = [sent], [moved(sent, 1)]
        for d in range(2, blocks, 2):
            held.append(moved(sent, d ^ (d in CROSSED)))
            theirs.append(moved(sent, d ^ (d not in CROSSED)) if d == 2 else moved(held[-1], 1))
        arrays = held + theirs
    else:
        arrays = [lax.all_gather(sent, "blk")]
    own = call(
        functools.partial(own_kernel, slab), shape(3, 8, B * B), after, velocity, near
    )
    room = (16 << 20) + (0 if paired else arrays[0].size * 4)
    out = call(
        functools.partial(last_kernel, slab, slabs, paired),
        shape(3, 1, 8, B * B),
        own,
        velocity,
        *arrays,
        params=pltpu.CompilerParams(vmem_limit_bytes=room),
    )
    return out[:, :, :slab]


def solution(mesh):
    return jax.shard_map(
        functools.partial(shards, mesh.shape["sub"]),
        mesh=mesh,
        in_specs=(
            P(None, "blk", "sub", None),
            P(None, "blk", "sub", None),
            P(None, "blk", "sub", None),
            P("blk", None),
        ),
        out_specs=P(None, "blk", "sub", None),
        check_vma=False,
    )
```
